128 devices in a mesh: row: 16 (over y, x), col: 8 (over z, core).
Axes of the slice: x: 4, y: 4, z: 4, core: 2. Of those that a mesh axis runs over, the one named last changes fastest.
Arguments:
- object_field: float32 [2, 4096, 8192], P(None, 'row', 'col'), may hold values from -5 to 5
- probe_modes: float32 [4, 2, 256, 256], replicated, may hold values from -4 to 4
- offsets: int32 [2, 384, 2], P(None, ('row', 'col')), may hold values from 0 to 7936, as said below
- live_counts: int32 [2, 128], P(None, ('row', 'col')), may hold values from 1 to 3, as said below
- patterns: float32 [2, 384, 256, 256], P(None, ('row', 'col')), may hold values from 0 to 4
Outputs:
- new_object: float32 [2, 4096, 8192], P(None, 'row', 'col')
- new_probe: float32 [4, 2, 256, 256], replicated
The draws below stay inside these ranges and needn't reach their ends.
Inputs may be any that keep to these rules, and one draw needn't show every extreme that they name: `offsets`: slots d * 3 to (d + 1) * 3 - 1 belong to device d (row-major over the mesh, d = row * 8 + col); each such slot's top-left pixel lies in that device's tile of 256 x 1024 pixels, and every window lies inside the object. Only the first live_counts[b, d] slots of device d are live in batch b; in every batch some device has exactly 3.
All inputs are finite; a program needn't handle non-finite values.
Results may differ from the reference program's by a relative error of at most 0.0003.
Values sent between devices are 32-bit elements; how exact they have to be, the bound alone decides.
A program may use at most 384 MiB of HBM per device.

```python
import jax
import jax.numpy as jnp
from jax import lax

W = 256
MODES = 4
TR = 256
TC = 1024
POS_CAP = 3
ITERS = 2
NR = 4096
NC = 8192
SLOTS = 384


def draw_offsets(key, part):
    key = jax.random.fold_in(key, 11)
    tile_count_cols = NC // TC
    slot_total = POS_CAP * (NR // TR) * tile_count_cols
    device = jnp.arange(slot_total, dtype=jnp.int32) // POS_CAP
    tile_row = device // tile_count_cols
    tile_col = device % tile_count_cols
    row_room = jnp.minimum(TR, NR - W - tile_row * TR + 1)
    col_room = jnp.minimum(TC, NC - W - tile_col * TC + 1)
    subkeys = jax.random.split(key, 2)
    row_local = jax.random.randint(subkeys[0], (ITERS, slot_total), 0, row_room[None, :])
    col_local = jax.random.randint(subkeys[1], (ITERS, slot_total), 0, col_room[None, :])
    rows_out = tile_row[None, :] * TR + row_local
    cols_out = tile_col[None, :] * TC + col_local
    last_first = slot_total - POS_CAP
    rows_out = rows_out.at[:, 0].set(0).at[:, last_first].set(NR - W)
    cols_out = cols_out.at[:, 0].set(0).at[:, last_first].set(NC - W)
    return jnp.stack([rows_out, cols_out], axis=-1).astype(jnp.int32)


def draw_live_counts(key, part):
    key = jax.random.fold_in(key, 23)
    devices = NR // TR * (NC // TC)
    subkeys = jax.random.split(key, 2)
    spread = jax.random.randint(subkeys[0], (ITERS, devices), 0, POS_CAP)
    counts = 1 + spread * spread // max(POS_CAP - 1, 1)
    busiest = jax.random.randint(subkeys[1], (ITERS, 1), 0, devices)
    device_ids = jnp.arange(devices, dtype=jnp.int32)[None, :]
    return jnp.where(device_ids == busiest, POS_CAP, counts).astype(jnp.int32)


def block_scale(stream_key, shape, pieces, smallest, largest):
    loudness, own = 1.0, jax.random.fold_in(stream_key, 6)
    for axis_at, blocks in pieces:
        draws = jnp.exp(jax.random.uniform(jax.random.fold_in(own, axis_at), (blocks,), jnp.float32, smallest / len(pieces), largest / len(pieces)))
        loudness = loudness * jnp.repeat(draws, shape[axis_at] // blocks).reshape([-1 if axis == axis_at else 1 for axis in range(len(shape))])
    return loudness


def gaussian(rng, extent, width, most, cuts=(), kind=jnp.bfloat16):
    array = width * jax.random.normal(rng, extent, jnp.float32)
    if cuts:
        array = array * block_scale(rng, extent, cuts, -0.22, 0.18)
    return jnp.clip(array, -most, most).astype(kind)


def setup_inputs(seed: int = 0) -> dict:
    key_of = jax.random.split(jax.random.key(seed), 6)
    object_field = gaussian(key_of[0], (2, NR, NC), 0.7, 5.0, ((1, 16), (2, 8)), jnp.float32)
    probe_modes = gaussian(key_of[1], (MODES, 2, W, W), 0.5, 4.0, (), jnp.float32)
    offsets = draw_offsets(jax.random.fold_in(key_of[5], 71), 0)
    live_counts = draw_live_counts(jax.random.fold_in(key_of[5], 71), 0)
    patterns = jnp.clip(4.0 * jax.random.uniform(key_of[4], (ITERS, SLOTS, W, W), jnp.float32) ** block_scale(key_of[4], (ITERS, SLOTS, W, W), ((1, 128),), -0.2, 0.2), 0.0, 4.0)
    return {"object_field": object_field, "probe_modes": probe_modes, "offsets": offsets, "live_counts": live_counts, "patterns": patterns}


step_object = 1.0
step_probe = 1.0
smoothing = 0.05
object_floor = 1.0
probe_floor = 0.001


def item_terms(window, pattern, probe_modes):
    probe_real = probe_modes[:, 0]
    probe_imag = probe_modes[:, 1]
    window_real = window[0]
    window_imag = window[1]
    wave_real = probe_real * window_real - probe_imag * window_imag
    wave_imag = probe_real * window_imag + probe_imag * window_real
    far_wave = jnp.fft.fft2(lax.complex(wave_real, wave_imag), norm="ortho")
    far_real = jnp.real(far_wave)
    far_imag = jnp.imag(far_wave)
    intensity = jnp.sum(far_real * far_real + far_imag * far_imag, axis=0)
    misfit = intensity - pattern
    back_wave = jnp.fft.ifft2(lax.complex(misfit * far_real, misfit * far_imag), norm="ortho")
    back_real = jnp.real(back_wave)
    back_imag = jnp.imag(back_wave)
    object_term = jnp.stack([jnp.sum(probe_real * back_real + probe_imag * back_imag, axis=0),
                             jnp.sum(probe_real * back_imag - probe_imag * back_real, axis=0)])
    probe_term = jnp.stack([window_real * back_real + window_imag * back_imag,
                            window_real * back_imag - window_imag * back_real], axis=1)
    window_power = window_real * window_real + window_imag * window_imag
    return object_term, probe_term, window_power


def laplacian(values):
    padded = jnp.pad(values, ((0, 0), (1, 1), (1, 1)))
    return padded[:, 2:, 1:-1] + padded[:, :-2, 1:-1] + padded[:, 1:-1, 2:] + padded[:, 1:-1, :-2] - 4.0 * values


def one_batch(object_field, probe_modes, spots, counts, pattern_set):
    slot_total = spots.shape[0]
    capacity = slot_total // counts.shape[0]
    side_len = probe_modes.shape[-1]
    slot_ids = jnp.arange(slot_total, dtype=jnp.int32)
    flags = (slot_ids % capacity < jnp.repeat(counts, capacity)).astype(jnp.float32)
    probe_power = jnp.sum(probe_modes * probe_modes, axis=(0, 1))

    def visit_item(state_now, record):
        gradient, weight, probe_grad, probe_weight = state_now
        location, pattern, live_flag = record
        row_at = location[0].astype(jnp.int32)
        col_at = location[1].astype(jnp.int32)
        zero_at = jnp.int32(0)
        window = lax.dynamic_slice(object_field, (zero_at, row_at, col_at), (2, side_len, side_len))
        object_term, probe_term, window_power = item_terms(window, pattern, probe_modes)
        current = lax.dynamic_slice(gradient, (zero_at, row_at, col_at), (2, side_len, side_len))
        gradient = lax.dynamic_update_slice(gradient, current + live_flag * object_term, (zero_at, row_at, col_at))
        covered = lax.dynamic_slice(weight, (row_at, col_at), (side_len, side_len))
        weight = lax.dynamic_update_slice(weight, covered + live_flag * probe_power, (row_at, col_at))
        return (gradient, weight, probe_grad + live_flag * probe_term, probe_weight + live_flag * window_power), None

    start_state = (jnp.zeros(object_field.shape, jnp.float32),
                   jnp.zeros(object_field.shape[1:], jnp.float32),
                   jnp.zeros(probe_modes.shape, jnp.float32),
                   jnp.zeros((side_len, side_len), jnp.float32))
    final_state, unused = lax.scan(visit_item, start_state, (spots, pattern_set, flags))
    gradient, weight, probe_grad, probe_weight = final_state
    new_object = object_field - step_object * gradient / (weight + object_floor) + step_object * smoothing * laplacian(object_field)
    new_probe = probe_modes - step_probe * probe_grad / (probe_weight + probe_floor)
    return new_object, new_probe


def reference(object_field, probe_modes, offsets, live_counts, patterns):
    for batch_index in range(ITERS):
        object_field, probe_modes = one_batch(object_field, probe_modes, offsets[batch_index],
                                              live_counts[batch_index], patterns[batch_index])
    return object_field, probe_modes
```

```python
import math

import jax
import jax.numpy as jnp
import ml_dtypes
import numpy as np
from jax import lax
from jax.experimental import pallas as pl
from jax.experimental.pallas import tpu as pltpu
from jax.sharding import PartitionSpec as P

step_object = 1.0
step_probe = 1.0
smoothing = 0.05
object_floor = 1.0
probe_floor = 0.001
SIDE = 256
HALF = 128
MODES = 4
VMEM = pltpu.VMEM
f32 = jnp.float32


def shifted(value, axis, steps):
    count = lax.axis_size(axis)
    leading, last = (max(0, -steps), min(count, count - steps))
    return lax.ppermute(value, axis, [(source, source + steps) for source in range(leading, last)])


def matrices():
    k, n = np.arange(HALF)[:, None], np.arange(HALF)[None, :]
    out = []
    for odd in (0, 1):
        angle = -2.0 * np.pi * (((2 * k + odd) * n) % SIDE) / SIDE
        re, im = np.cos(angle) / math.sqrt(SIDE), np.sin(angle) / math.sqrt(SIDE)
        big = np.block([[re, -im], [im, re]])
        for matrix in (big, big.T):
            high = matrix.astype(ml_dtypes.bfloat16)
            low = (matrix - high.astype(np.float64)).astype(ml_dtypes.bfloat16)
            out += [high, low]
    return np.stack(out)


def split(value):
    high = value.astype(jnp.bfloat16)
    return high, (value - high.astype(f32)).astype(jnp.bfloat16)


def dot(a, b):
    return jnp.dot(a, b, preferred_element_type=f32)


def left(mats, index, value):
    high, low = split(value)
    a, b = mats[index], mats[index + 1]
    return dot(a, high) + dot(b, high) + dot(a, low)


def right(value, mats, index):
    high, low = split(value)
    a, b = mats[index], mats[index + 1]
    return dot(high, a) + dot(high, b) + dot(low, a)


def cat(axis, *values):
    return jnp.concatenate(values, axis=axis)


def iotas():
    shape = (SIDE, SIDE)
    return lax.broadcasted_iota(jnp.int32, shape, 0), lax.broadcasted_iota(jnp.int32, shape, 1)


def roll2(value, rows, cols):
    return pltpu.roll(pltpu.roll(value, rows, 0), cols, 1)


def pattern_kernel(pat_ref, perm_ref, out_ref):
    high, low = split(pat_ref[0])
    value = dot(perm_ref[0], high) + dot(perm_ref[0], low)
    high, low = split(value)
    out_ref[0] = dot(high, perm_ref[1]) + dot(low, perm_ref[1])


def order_patterns(patterns):
    perm = np.zeros((SIDE, SIDE), np.float32)
    j = np.arange(SIDE)
    perm[j, (j % 2) * HALF + j // 2] = 1.0
    count = patterns.shape[0]
    block = pl.BlockSpec((1, SIDE, SIDE), lambda i: (i, 0, 0))
    return pl.pallas_call(
        pattern_kernel,
        grid=(count,),
        in_specs=[block, pl.BlockSpec((2, SIDE, SIDE), lambda i: (0, 0, 0))],
        out_specs=block,
        out_shape=jax.ShapeDtypeStruct(patterns.shape, f32),
        name="order_patterns",
    )(patterns, jnp.asarray(np.stack([perm.T, perm]), jnp.bfloat16))


def pack_kernel(last, sc, a_ref, b_ref, rim_ref, out_ref):
    _, cols = iotas()
    cm = sc[2]
    for part in range(2):
        after = jnp.where(sc[0] == last, rim_ref[part], b_ref[part])
        out_ref[part] = jnp.where(cols >= cm, a_ref[part], after)


def tile_specs(last):
    part = lambda index: pl.BlockSpec((2, SIDE, SIDE), index)
    return [
        part(lambda i, sc: (0, 0, sc[0])),
        part(lambda i, sc: (0, 0, jnp.minimum(sc[0] + 1, last))),
        part(lambda i, sc: (0, 0, 0)),
    ]


def pack(info, tile, rim):
    last = tile.shape[2] // SIDE - 1
    return pl.pallas_call(
        lambda *refs: pack_kernel(last, *refs),
        grid_spec=pltpu.PrefetchScalarGridSpec(
            num_scalar_prefetch=1,
            grid=(1,),
            in_specs=tile_specs(last),
            out_specs=pl.BlockSpec((2, SIDE, SIDE), lambda i, sc: (0, 0, 0)),
        ),
        out_shape=jax.ShapeDtypeStruct((2, SIDE, SIDE), f32),
        name="pack",
    )(info, tile, tile, rim)


def slot_kernel(last, first, sc, a_ref, b_ref, rim_ref, below_ref, pat_ref, probe_ref, mats, *refs):
    if first:
        w_ref, pg_ref, psi = refs
    else:
        pg_in, w_ref, pg_ref, psi = refs
    r, cm, live = sc[1], sc[2], sc[3]

    @pl.when(live == 0)
    def _():
        w_ref[...] = jnp.zeros_like(w_ref)
        if first:
            pg_ref[...] = jnp.zeros_like(pg_ref)
        else:
            pg_ref[...] = pg_in[...]

    @pl.when(live == 1)
    def _():
        rows, cols = iotas()
        window = []
        for part in range(2):
            after = jnp.where(sc[0] == last, rim_ref[part], b_ref[part])
            own = jnp.where(cols >= cm, a_ref[part], after)
            whole = jnp.where(rows >= r, own, below_ref[part])
            window.append(roll2(whole, lax.rem(SIDE - r, SIDE), lax.rem(SIDE - cm, SIDE)))
        xr, xi = window
        total_e = total_o = None
        for m in range(MODES):
            pr, pi = probe_ref[m, 0], probe_ref[m, 1]
            wr, wi = pr * xr - pi * xi, pr * xi + pi * xr
            even = left(mats, 0, cat(0, wr[:HALF] + wr[HALF:], wi[:HALF] + wi[HALF:]))
            odd = left(mats, 4, cat(0, wr[:HALF] - wr[HALF:], wi[:HALF] - wi[HALF:]))
            tr, ti = cat(0, even[:HALF], odd[:HALF]), cat(0, even[HALF:], odd[HALF:])
            pe = right(cat(1, tr[:, :HALF] + tr[:, HALF:], ti[:, :HALF] + ti[:, HALF:]), mats, 2)
            po = right(cat(1, tr[:, :HALF] - tr[:, HALF:], ti[:, :HALF] - ti[:, HALF:]), mats, 6)
            psi[m, 0], psi[m, 1] = pe, po
            total_e = pe * pe if m == 0 else total_e + pe * pe
            total_o = po * po if m == 0 else total_o + po * po
        de = total_e[:, :HALF] + total_e[:, HALF:] - pat_ref[0, :, :HALF]
        do = total_o[:, :HALF] + total_o[:, HALF:] - pat_ref[0, :, HALF:]
        de, do = cat(1, de, de), cat(1, do, do)
        grad_r = grad_i = None
        for m in range(MODES):
            ue, uo = right(psi[m, 0] * de, mats, 0), right(psi[m, 1] * do, mats, 4)
            plus, minus = ue + uo, ue - uo
            tr, ti = cat(1, plus[:, :HALF], minus[:, :HALF]), cat(1, plus[:, HALF:], minus[:, HALF:])
            ze = left(mats, 2, cat(0, tr[:HALF], ti[:HALF]))
            zo = left(mats, 6, cat(0, tr[HALF:], ti[HALF:]))
            plus, minus = ze + zo, ze - zo
            br, bi = cat(0, plus[:HALF], minus[:HALF]), cat(0, plus[HALF:], minus[HALF:])
            pr, pi = probe_ref[m, 0], probe_ref[m, 1]
            gr, gi = pr * br + pi * bi, pr * bi - pi * br
            grad_r = gr if m == 0 else grad_r + gr
            grad_i = gi if m == 0 else grad_i + gi
            tr, ti = xr * br + xi * bi, xr * bi - xi * br
            pg_ref[2 * m] = tr if first else pg_in[2 * m] + tr
            pg_ref[2 * m + 1] = ti if first else pg_in[2 * m + 1] + ti
        power = xr * xr + xi * xi
        pg_ref[2 * MODES] = power if first else pg_in[2 * MODES] + power
        w_ref[0] = roll2(grad_r, r, cm)
        w_ref[1] = roll2(grad_i, r, cm)


def run_slot(info, slot, tile, rim, below, patterns, probe, mats, pg):
    last = tile.shape[2] // SIDE - 1
    first = pg is None
    whole = lambda shape: pl.BlockSpec(shape, lambda i, sc: (0,) * len(shape))
    pg_shape = (2 * MODES + 1, SIDE, SIDE)
    return pl.pallas_call(
        lambda *refs: slot_kernel(last, first, *refs),
        grid_spec=pltpu.PrefetchScalarGridSpec(
            num_scalar_prefetch=1,
            grid=(1,),
            in_specs=tile_specs(last)
            + [
                whole((2, SIDE, SIDE)),
                pl.BlockSpec((1, SIDE, SIDE), lambda i, sc: (slot, 0, 0)),
                whole(probe.shape),
                whole(mats.shape),
            ]
            + ([] if first else [whole(pg_shape)]),
            out_specs=[whole((2, SIDE, SIDE)), whole(pg_shape)],
            scratch_shapes=[pltpu.VMEM((MODES, 2, SIDE, SIDE), f32)],
        ),
        out_shape=[
            jax.ShapeDtypeStruct((2, SIDE, SIDE), f32),
            jax.ShapeDtypeStruct(pg_shape, f32),
        ],
        compiler_params=pltpu.CompilerParams(vmem_limit_bytes=40 * 2**20),
        cost_estimate=pl.CostEstimate(flops=2 * 96 * SIDE**3, bytes_accessed=8 * 2**20, transcendentals=0),
        name="slot",
    )(info, tile, tile, rim, below, patterns, probe, mats, *([] if first else [pg]))


def prepare_kernel(sc, tile, above, below, before, rim, probe_ref, base_ref, weight_ref):
    chunks = weight_ref.shape[0]
    rows, cols = iotas()
    power = probe_ref[0, 0] * probe_ref[0, 0]
    for m in range(MODES):
        for part in range(2):
            if m or part:
                power = power + probe_ref[m, part] * probe_ref[m, part]
    weight_ref[...] = jnp.zeros_like(weight_ref)
    count = sc.shape[1]
    for where in range(4):
        for slot in range(count):
            k, r, cm, live = [sc[where, slot, j] for j in range(4)]
            is_left = where >= 2

            @pl.when((live == 1) & ((k == chunks - 1) if is_left else True))
            def _():
                value = roll2(power, r, cm)
                inside = (rows >= r) if where % 2 == 0 else (rows < r)
                value = jnp.where(inside, value, 0.0)
                if is_left:
                    weight_ref[0] += jnp.where(cols < cm, value, 0.0)
                else:
                    weight_ref[k] += jnp.where(cols >= cm, value, 0.0)

                    @pl.when(k < chunks - 1)
                    def _():
                        weight_ref[k + 1] += jnp.where(cols < cm, value, 0.0)

    height, width = tile.shape[1:]
    row_at = lax.broadcasted_iota(jnp.int32, (height, width), 0)
    col_at = lax.broadcasted_iota(jnp.int32, (height, width), 1)
    for part in range(2):
        here = tile[part]
        up = jnp.where(row_at == 0, above[part, 7:8, :], pltpu.roll(here, 1, 0))
        down = jnp.where(row_at == height - 1, below[part, 0:1, :], pltpu.roll(here, height - 1, 0))
        lhs = jnp.where(col_at == 0, before[part, :, HALF - 1 : HALF], pltpu.roll(here, 1, 1))
        rhs = jnp.where(col_at == width - 1, rim[part, :, 0:1], pltpu.roll(here, width - 1, 1))
        neighbours = up + down + lhs + rhs
        base_ref[part] = here + (step_object * smoothing) * (neighbours - 4.0 * here)


def prepare(infos, tile, rim, probe):
    above = shifted(tile[:, -8:, :], "row", 1)
    below = shifted(tile[:, :8, :], "row", -1)
    before = shifted(tile[:, :, -HALF:], "col", 1)
    chunks = tile.shape[2] // SIDE
    vmem = pl.BlockSpec(memory_space=VMEM)
    return pl.pallas_call(
        prepare_kernel,
        in_specs=[pl.BlockSpec(memory_space=pltpu.SMEM)] + [vmem] * 6,
        out_specs=[vmem, vmem],
        out_shape=[
            jax.ShapeDtypeStruct(tile.shape, f32),
            jax.ShapeDtypeStruct((chunks, SIDE, SIDE), f32),
        ],
        compiler_params=pltpu.CompilerParams(vmem_limit_bytes=40 * 2**20),
        cost_estimate=pl.CostEstimate(flops=2**25, bytes_accessed=8 * 2**20, transcendentals=0),
        name="prepare",
    )(infos, tile, above, below, before, rim, probe)


def gather_kernel(sc, *refs):
    acc = refs[-1]
    acc[...] = jnp.zeros_like(acc)
    rows, cols = iotas()
    count = sc.shape[1]
    for where in range(2):
        for slot in range(count):
            k, r, cm, live = [sc[where, slot, j] for j in range(4)]
            ref = refs[where * count + slot]

            @pl.when(live == 1)
            def _():
                inside = (rows >= r) if where == 0 else (rows < r)
                for part in range(2):
                    value = jnp.where(inside, ref[part], 0.0)
                    acc[k, part] += jnp.where(cols >= cm, value, 0.0)
                    acc[k + 1, part] += jnp.where(cols < cm, value, 0.0)


def gather(infos, own, arrived, chunks):
    vmem = pl.BlockSpec(memory_space=VMEM)
    return pl.pallas_call(
        gather_kernel,
        in_specs=[pl.BlockSpec(memory_space=pltpu.SMEM)] + [vmem] * (len(own) + len(arrived)),
        out_specs=vmem,
        out_shape=jax.ShapeDtypeStruct((chunks + 1, 2, SIDE, SIDE), f32),
        compiler_params=pltpu.CompilerParams(vmem_limit_bytes=40 * 2**20),
        name="gather",
    )(infos, *own, *arrived)


def update_kernel(base, acc, weight, extra, out):
    scale = step_object / (weight[0] + object_floor)

    @pl.when(pl.program_id(0) == 0)
    def _():
        for part in range(2):
            out[part] = base[part] - scale * (acc[0, part] + extra[part])

    @pl.when(pl.program_id(0) > 0)
    def _():
        for part in range(2):
            out[part] = base[part] - scale * acc[0, part]


def update(base, acc, weight, extra):
    chunks = weight.shape[0]
    tile = pl.BlockSpec((2, SIDE, SIDE), lambda i: (0, 0, i))
    return pl.pallas_call(
        update_kernel,
        grid=(chunks,),
        in_specs=[
            tile,
            pl.BlockSpec((1, 2, SIDE, SIDE), lambda i: (i, 0, 0, 0)),
            pl.BlockSpec((1, SIDE, SIDE), lambda i: (i, 0, 0)),
            pl.BlockSpec((2, SIDE, SIDE), lambda i: (0, 0, 0)),
        ],
        out_specs=tile,
        out_shape=jax.ShapeDtypeStruct(base.shape, f32),
        name="update",
    )(base, acc, weight, extra)


def shards(object_field, probe_modes, offsets, live_counts, patterns):
    tile_rows, tile_cols = object_field.shape[1:]
    chunks = tile_cols // SIDE
    batches, capacity = offsets.shape[:2]
    mats = jnp.asarray(matrices())
    anchor = jnp.stack([lax.axis_index("row") * tile_rows, lax.axis_index("col") * tile_cols])
    local = offsets - anchor[None, None, :]
    row_at, col_at = local[..., 0], local[..., 1]
    live = (jnp.arange(capacity)[None, :] < live_counts).astype(jnp.int32)
    own = jnp.stack([col_at // SIDE, row_at, col_at % SIDE, live], axis=-1)
    two = jnp.stack([own, shifted(own, "row", 1)], axis=1)
    infos = jnp.concatenate([two, shifted(two, "col", 1)], axis=1)
    ordered = [order_patterns(patterns[b]) for b in range(batches)]

    tile, probe = object_field, probe_modes
    rim = shifted(tile[:, :, :SIDE], "col", -1)
    for b in range(batches):
        info = infos[b]
        below = [shifted(pack(info[1, s], tile, rim), "row", -1) for s in range(capacity)]
        base, weight = prepare(info, tile, rim, probe)
        if b + 1 < batches:
            side = jnp.concatenate([base[:, :, :SIDE], weight[:1]], axis=0)
            side = shifted(side, "col", -1)
        pg, own_grads, arrived = None, [], []
        for s in range(capacity):
            grad, pg = run_slot(info[0, s], s, tile, rim, below[s], ordered[b], probe, mats, pg)
            own_grads.append(grad)
            arrived.append(shifted(grad, "row", 1))
        acc = gather(info, own_grads, arrived, chunks)
        from_left = shifted(acc[chunks], "col", 1)
        if b + 1 < batches:
            from_right = shifted(acc[0], "col", -1)
            rim = side[:2] - step_object * (acc[chunks] + from_right) / (side[2] + object_floor)
        tile = update(base, acc, weight, from_left)
        total = lax.psum(pg, ("row", "col"))
        step = step_probe * total[: 2 * MODES] / (total[2 * MODES] + probe_floor)
        probe = probe - step.reshape(probe.shape)
    return (tile, probe)


def solution(mesh):
    placed = (
        P(None, "row", "col"),
        P(),
        P(None, ("row", "col"), None),
        P(None, ("row", "col")),
        P(None, ("row", "col"), None, None),
    )
    return jax.shard_map(
        shards, mesh=mesh, in_specs=placed, out_specs=(P(None, "row", "col"), P()), check_vma=False
    )
```

```python
import math

import jax
import jax.numpy as jnp
import ml_dtypes
import numpy as np
from jax import lax
from jax.experimental import pallas as pl
from jax.experimental.pallas import tpu as pltpu
from jax.sharding import PartitionSpec as P

step_object = 1.0
step_probe = 1.0
smoothing = 0.05
object_floor = 1.0
probe_floor = 0.001
SIDE = 256
HALF = 128
MODES = 4
VMEM = pltpu.VMEM
f32 = jnp.float32


def shifted(value, axis, steps):
    count = lax.axis_size(axis)
    leading, last = (max(0, -steps), min(count, count - steps))
    return lax.ppermute(value, axis, [(source, source + steps) for source in range(leading, last)])


def matrices():
    k, n = np.arange(HALF)[:, None], np.arange(HALF)[None, :]
    out = []
    for odd in (0, 1):
        angle = -2.0 * np.pi * (((2 * k + odd) * n) % SIDE) / SIDE
        re, im = np.cos(angle) / math.sqrt(SIDE), np.sin(angle) / math.sqrt(SIDE)
        big = np.block([[re, -im], [im, re]])
        for matrix in (big, big.T):
            high = matrix.astype(ml_dtypes.bfloat16)
            low = (matrix - high.astype(np.float64)).astype(ml_dtypes.bfloat16)
            out += [high, low]
    return np.stack(out)


def split(value):
    high = value.astype(jnp.bfloat16)
    return high, (value - high.astype(f32)).astype(jnp.bfloat16)


def dot(a, b):
    return jnp.dot(a, b, preferred_element_type=f32)


def left(mats, index, value):
    high, low = split(value)
    a, b = mats[index], mats[index + 1]
    return dot(a, high) + dot(b, high) + dot(a, low)


def right(value, mats, index):
    high, low = split(value)
    a, b = mats[index], mats[index + 1]
    return dot(high, a) + dot(high, b) + dot(low, a)


def cat(axis, *values):
    return jnp.concatenate(values, axis=axis)


def iotas():
    shape = (SIDE, SIDE)
    return lax.broadcasted_iota(jnp.int32, shape, 0), lax.broadcasted_iota(jnp.int32, shape, 1)


def roll2(value, rows, cols):
    return pltpu.roll(pltpu.roll(value, rows, 0), cols, 1)


def pattern_kernel(pat_ref, perm_ref, out_ref):
    high, low = split(pat_ref[0])
    value = dot(perm_ref[0], high) + dot(perm_ref[0], low)
    high, low = split(value)
    out_ref[0] = dot(high, perm_ref[1]) + dot(low, perm_ref[1])


def order_patterns(patterns):
    perm = np.zeros((SIDE, SIDE), np.float32)
    j = np.arange(SIDE)
    perm[j, (j % 2) * HALF + j // 2] = 1.0
    count = patterns.shape[0]
    block = pl.BlockSpec((1, SIDE, SIDE), lambda i: (i, 0, 0))
    return pl.pallas_call(
        pattern_kernel,
        grid=(count,),
        in_specs=[block, pl.BlockSpec((2, SIDE, SIDE), lambda i: (0, 0, 0))],
        out_specs=block,
        out_shape=jax.ShapeDtypeStruct(patterns.shape, f32),
        name="order_patterns",
    )(patterns, jnp.asarray(np.stack([perm.T, perm]), jnp.bfloat16))


def pack_kernel(last, sc, a_ref, b_ref, rim_ref, out_ref):
    _, cols = iotas()
    cm = sc[2]
    for part in range(2):
        after = jnp.where(sc[0] == last, rim_ref[part], b_ref[part])
        out_ref[part] = jnp.where(cols >= cm, a_ref[part], after)


def tile_specs(last):
    part = lambda index: pl.BlockSpec((2, SIDE, SIDE), index)
    return [
        part(lambda i, sc: (0, 0, sc[0])),
        part(lambda i, sc: (0, 0, jnp.minimum(sc[0] + 1, last))),
        part(lambda i, sc: (0, 0, 0)),
    ]


def pack(info, tile, rim):
    last = tile.shape[2] // SIDE - 1
    return pl.pallas_call(
        lambda *refs: pack_kernel(last, *refs),
        grid_spec=pltpu.PrefetchScalarGridSpec(
            num_scalar_prefetch=1,
            grid=(1,),
            in_specs=tile_specs(last),
            out_specs=pl.BlockSpec((2, SIDE, SIDE), lambda i, sc: (0, 0, 0)),
        ),
        out_shape=jax.ShapeDtypeStruct((2, SIDE, SIDE), f32),
        name="pack",
    )(info, tile, tile, rim)


def slot_kernel(last, first, sc, a_ref, b_ref, rim_ref, below_ref, pat_ref, probe_ref, mats, *refs):
    if first:
        w_ref, pg_ref, psi = refs
    else:
        pg_in, w_ref, pg_ref, psi = refs
    r, cm, live = sc[1], sc[2], sc[3]

    @pl.when(live == 0)
    def _():
        w_ref[...] = jnp.zeros_like(w_ref)
        if first:
            pg_ref[...] = jnp.zeros_like(pg_ref)
        else:
            pg_ref[...] = pg_in[...]

    @pl.when(live == 1)
    def _():
        rows, cols = iotas()
        window = []
        for part in range(2):
            after = jnp.where(sc[0] == last, rim_ref[part], b_ref[part])
            own = jnp.where(cols >= cm, a_ref[part], after)
            whole = jnp.where(rows >= r, own, below_ref[part])
            window.append(roll2(whole, lax.rem(SIDE - r, SIDE), lax.rem(SIDE - cm, SIDE)))
        xr, xi = window
        total_e = total_o = None
        for m in range(MODES):
            pr, pi = probe_ref[m, 0], probe_ref[m, 1]
            wr, wi = pr * xr - pi * xi, pr * xi + pi * xr
            even = left(mats, 0, cat(0, wr[:HALF] + wr[HALF:], wi[:HALF] + wi[HALF:]))
            odd = left(mats, 4, cat(0, wr[:HALF] - wr[HALF:], wi[:HALF] - wi[HALF:]))
            tr, ti = cat(0, even[:HALF], odd[:HALF]), cat(0, even[HALF:], odd[HALF:])
            pe = right(cat(1, tr[:, :HALF] + tr[:, HALF:], ti[:, :HALF] + ti[:, HALF:]), mats, 2)
            po = right(cat(1, tr[:, :HALF] - tr[:, HALF:], ti[:, :HALF] - ti[:, HALF:]), mats, 6)
            psi[m, 0], psi[m, 1] = pe, po
            total_e = pe * pe if m == 0 else total_e + pe * pe
            total_o = po * po if m == 0 else total_o + po * po
        de = total_e[:, :HALF] + total_e[:, HALF:] - pat_ref[0, :, :HALF]
        do = total_o[:, :HALF] + total_o[:, HALF:] - pat_ref[0, :, HALF:]
        de, do = cat(1, de, de), cat(1, do, do)
        grad_r = grad_i = None
        for m in range(MODES):
            ue, uo = right(psi[m, 0] * de, mats, 0), right(psi[m, 1] * do, mats, 4)
            plus, minus = ue + uo, ue - uo
            tr, ti = cat(1, plus[:, :HALF], minus[:, :HALF]), cat(1, plus[:, HALF:], minus[:, HALF:])
            ze = left(mats, 2, cat(0, tr[:HALF], ti[:HALF]))
            zo = left(mats, 6, cat(0, tr[HALF:], ti[HALF:]))
            plus, minus = ze + zo, ze - zo
            br, bi = cat(0, plus[:HALF], minus[:HALF]), cat(0, plus[HALF:], minus[HALF:])
            pr, pi = probe_ref[m, 0], probe_ref[m, 1]
            gr, gi = pr * br + pi * bi, pr * bi - pi * br
            grad_r = gr if m == 0 else grad_r + gr
            grad_i = gi if m == 0 else grad_i + gi
            tr, ti = xr * br + xi * bi, xr * bi - xi * br
            pg_ref[2 * m] = tr if first else pg_in[2 * m] + tr
            pg_ref[2 * m + 1] = ti if first else pg_in[2 * m + 1] + ti
        power = xr * xr + xi * xi
        pg_ref[2 * MODES] = power if first else pg_in[2 * MODES] + power
        w_ref[0] = roll2(grad_r, r, cm)
        w_ref[1] = roll2(grad_i, r, cm)


def run_slot(info, slot, tile, rim, below, patterns, probe, mats, pg):
    last = tile.shape[2] // SIDE - 1
    first = pg is None
    whole = lambda shape: pl.BlockSpec(shape, lambda i, sc: (0,) * len(shape))
    pg_shape = (2 * MODES + 1, SIDE, SIDE)
    return pl.pallas_call(
        lambda *refs: slot_kernel(last, first, *refs),
        grid_spec=pltpu.PrefetchScalarGridSpec(
            num_scalar_prefetch=1,
            grid=(1,),
            in_specs=tile_specs(last)
            + [
                whole((2, SIDE, SIDE)),
                pl.BlockSpec((1, SIDE, SIDE), lambda i, sc: (slot, 0, 0)),
                whole(probe.shape),
                whole(mats.shape),
            ]
            + ([] if first else [whole(pg_shape)]),
            out_specs=[whole((2, SIDE, SIDE)), whole(pg_shape)],
            scratch_shapes=[pltpu.VMEM((MODES, 2, SIDE, SIDE), f32)],
        ),
        out_shape=[
            jax.ShapeDtypeStruct((2, SIDE, SIDE), f32),
            jax.ShapeDtypeStruct(pg_shape, f32),
        ],
        compiler_params=pltpu.CompilerParams(vmem_limit_bytes=40 * 2**20),
        cost_estimate=pl.CostEstimate(flops=2 * 96 * SIDE**3, bytes_accessed=8 * 2**20, transcendentals=0),
        name="slot",
    )(info, tile, tile, rim, below, patterns, probe, mats, *([] if first else [pg]))


def prepare_kernel(sc, tile, above, below, before, rim, probe_ref, base_ref, weight_ref):
    chunks = weight_ref.shape[0]
    rows, cols = iotas()
    power = probe_ref[0, 0] * probe_ref[0, 0]
    for m in range(MODES):
        for part in range(2):
            if m or part:
                power = power + probe_ref[m, part] * probe_ref[m, part]
    weight_ref[...] = jnp.zeros_like(weight_ref)
    count = sc.shape[1]
    for where in range(4):
        for slot in range(count):
            k, r, cm, live = [sc[where, slot, j] for j in range(4)]
            is_left = where >= 2

            @pl.when((live == 1) & ((k == chunks - 1) if is_left else True))
            def _():
                value = roll2(power, r, cm)
                inside = (rows >= r) if where % 2 == 0 else (rows < r)
                value = jnp.where(inside, value, 0.0)
                if is_left:
                    weight_ref[0] += jnp.where(cols < cm, value, 0.0)
                else:
                    weight_ref[k] += jnp.where(cols >= cm, value, 0.0)

                    @pl.when(k < chunks - 1)
                    def _():
                        weight_ref[k + 1] += jnp.where(cols < cm, value, 0.0)

    height, width = tile.shape[1:]
    row_at = lax.broadcasted_iota(jnp.int32, (height, width), 0)
    col_at = lax.broadcasted_iota(jnp.int32, (height, width), 1)
    for part in range(2):
        here = tile[part]
        up = jnp.where(row_at == 0, above[part, 7:8, :], pltpu.roll(here, 1, 0))
        down = jnp.where(row_at == height - 1, below[part, 0:1, :], pltpu.roll(here, height - 1, 0))
        lhs = jnp.where(col_at == 0, before[part, :, HALF - 1 : HALF], pltpu.roll(here, 1, 1))
        rhs = jnp.where(col_at == width - 1, rim[part, :, 0:1], pltpu.roll(here, width - 1, 1))
        neighbours = up + down + lhs + rhs
        base_ref[part] = here + (step_object * smoothing) * (neighbours - 4.0 * here)


def prepare(infos, tile, rim, probe):
    above = shifted(tile[:, -8:, :], "row", 1)
    below = shifted(tile[:, :8, :], "row", -1)
    before = shifted(tile[:, :, -HALF:], "col", 1)
    chunks = tile.shape[2] // SIDE
    vmem = pl.BlockSpec(memory_space=VMEM)
    return pl.pallas_call(
        prepare_kernel,
        in_specs=[pl.BlockSpec(memory_space=pltpu.SMEM)] + [vmem] * 6,
        out_specs=[vmem, vmem],
        out_shape=[
            jax.ShapeDtypeStruct(tile.shape, f32),
            jax.ShapeDtypeStruct((chunks, SIDE, SIDE), f32),
        ],
        compiler_params=pltpu.CompilerParams(vmem_limit_bytes=40 * 2**20),
        cost_estimate=pl.CostEstimate(flops=2**25, bytes_accessed=8 * 2**20, transcendentals=0),
        name="prepare",
    )(infos, tile, above, below, before, rim, probe)


def gather_kernel(sc, *refs):
    acc = refs[-1]
    acc[...] = jnp.zeros_like(acc)
    rows, cols = iotas()
    count = sc.shape[1]
    for where in range(2):
        for slot in range(count):
            k, r, cm, live = [sc[where, slot, j] for j in range(4)]
            ref = refs[where * count + slot]

            @pl.when(live == 1)
            def _():
                inside = (rows >= r) if where == 0 else (rows < r)
                for part in range(2):
                    value = jnp.where(inside, ref[part], 0.0)
                    acc[k, part] += jnp.where(cols >= cm, value, 0.0)
                    acc[k + 1, part] += jnp.where(cols < cm, value, 0.0)


def gather(infos, own, arrived, chunks):
    vmem = pl.BlockSpec(memory_space=VMEM)
    return pl.pallas_call(
        gather_kernel,
        in_specs=[pl.BlockSpec(memory_space=pltpu.SMEM)] + [vmem] * (len(own) + len(arrived)),
        out_specs=vmem,
        out_shape=jax.ShapeDtypeStruct((chunks + 1, 2, SIDE, SIDE), f32),
        compiler_params=pltpu.CompilerParams(vmem_limit_bytes=40 * 2**20),
        name="gather",
    )(infos, *own, *arrived)


def update_kernel(base, acc, weight, extra, out):
    scale = step_object / (weight[0] + object_floor)

    @pl.when(pl.program_id(0) == 0)
    def _():
        for part in range(2):
            out[part] = base[part] - scale * (acc[0, part] + extra[part])

    @pl.when(pl.program_id(0) > 0)
    def _():
        for part in range(2):
            out[part] = base[part] - scale * acc[0, part]


def update(base, acc, weight, extra):
    chunks = weight.shape[0]
    tile = pl.BlockSpec((2, SIDE, SIDE), lambda i: (0, 0, i))
    return pl.pallas_call(
        update_kernel,
        grid=(chunks,),
        in_specs=[
            tile,
            pl.BlockSpec((1, 2, SIDE, SIDE), lambda i: (i, 0, 0, 0)),
            pl.BlockSpec((1, SIDE, SIDE), lambda i: (i, 0, 0)),
            pl.BlockSpec((2, SIDE, SIDE), lambda i: (0, 0, 0)),
        ],
        out_specs=tile,
        out_shape=jax.ShapeDtypeStruct(base.shape, f32),
        name="update",
    )(base, acc, weight, extra)


MESH = pl.DeviceIdType.MESH
PLANES = 2 * MODES + 1


def place():
    row, col = lax.axis_index("row"), lax.axis_index("col")
    return lax.div(row, 4), lax.rem(row, 4), lax.div(col, 2), lax.rem(col, 2)


def device(y, x, z, core):
    return (y * 4 + x, z * 2 + core)


def peers(y, x, z, core, axis, step):
    if axis == "core":
        return device(y, x, z, 1 - core)
    if axis == "x":
        return device(y, lax.rem(x + step, 4), z, core)
    along_y = (1 - core) if axis == "first" else core
    return device(lax.rem(y + step * along_y, 4), x, lax.rem(z + step * (1 - along_y), 4), core)


def meet(here, axes):
    barrier = pltpu.get_barrier_semaphore()
    who = [peers(*here, axis, step) for axis in axes for step in ((1,) if axis == "core" else (1, 2, 3))]
    for device_id in who:
        pl.semaphore_signal(barrier, inc=1, device_id=device_id, device_id_type=MESH)
    pl.semaphore_wait(barrier, len(who))


def remote(src, dst, send, recv, device_id):
    return pltpu.make_async_remote_copy(
        src_ref=src, dst_ref=dst, send_sem=send, recv_sem=recv, device_id=device_id, device_id_type=MESH
    )


def reduce_kernel(pg, probe, out, half, got1, got2, got3, got4, send, recv):
    here = y, x, z, core = place()
    first, second = y + core * (z - y), z + core * (y - z)
    meet(here, ("core", "first", "second", "x"))
    sibling = peers(*here, "core", 1)
    order = [lax.rem(first + step, 4) for step in (2, 1, 3, 0)]
    at = lambda base, index, size: pl.ds(pl.multiple_of(base + index * size, 8), size)
    ones = []
    for i, piece in enumerate(order):
        theirs = at((1 - core) * HALF, lax.rem(second + (2, 1, 3, 0)[i], 4), 32)
        there = at(0, lax.rem(second + (2, 1, 3, 0)[i], 4), 32)
        copy = remote(pg.at[:, theirs, :], got1.at[:, there, :], send.at[i], recv.at[i], sibling)
        copy.start()
        ones.append(copy)
    twos = []
    for i, piece in enumerate(order):
        ones[i].wait_recv()
        mine, there = at(core * HALF, piece, 32), at(0, piece, 32)
        half[:, there, :] = pg[:, mine, :] + got1[:, there, :]
        if i < 3:
            step = (2, 1, 3)[i]
            copy = remote(
                half.at[:, there, :], got2.at[step - 1], send.at[4 + i], recv.at[4 + i], peers(*here, "first", step)
            )
            copy.start()
            twos.append(copy)
    for copy in twos:
        copy.wait_recv()
    start = first * 32
    threes = []
    for i, step in enumerate((2, 1, 3, 0)):
        piece = lax.rem(second + step, 4)
        rows, within = at(start, piece, 8), at(0, piece, 8)
        half[:, rows, :] = half[:, rows, :] + got2[0, :, within, :] + got2[1, :, within, :] + got2[2, :, within, :]
        if step:
            copy = remote(
                half.at[:, rows, :], got3.at[step - 1], send.at[7 + i], recv.at[7 + i], peers(*here, "second", step)
            )
            copy.start()
            threes.append(copy)
    for copy in threes:
        copy.wait_recv()
    rows = at(start, second, 8)
    got4[x] = half[:, rows, :] + got3[0] + got3[1] + got3[2]
    fours = []
    for i, step in enumerate((2, 1, 3)):
        copy = remote(got4.at[x], got4.at[x], send.at[10 + i], recv.at[10 + i], peers(*here, "x", step))
        copy.start()
        fours.append(copy)
    for copy in fours:
        copy.wait_recv()
    total = got4[0] + got4[1] + got4[2] + got4[3]
    scale = step_probe / (total[2 * MODES] + probe_floor)
    mine = at(core * HALF + start, second, 8)
    for plane in range(2 * MODES):
        out[plane] = probe[plane, mine, :] - scale * total[plane]
    for copy in ones + twos + threes + fours:
        copy.wait_send()


def spread_kernel(shard, out, send, recv):
    here = y, x, z, core = place()
    first, second = y + core * (z - y), z + core * (y - z)
    meet(here, ("core", "first", "second"))
    at = lambda base, index, size: out.at[:, pl.ds(pl.multiple_of(base + index * size, 8), size), :]
    base = core * HALF
    mine = base + first * 32 + second * 8
    out[:, pl.ds(pl.multiple_of(mine, 8), 8), :] = shard[...]
    copies = []
    for i, step in enumerate((2, 1, 3)):
        block = at(mine, 0, 8)
        copy = remote(block, block, send.at[i], recv.at[i], peers(*here, "second", step))
        copy.start()
        copies.append(copy)
    for copy in copies:
        copy.wait_recv()
    whole = at(base, first, 32)
    twos = []
    for i, step in enumerate((2, 1, 3)):
        copy = remote(whole, whole, send.at[3 + i], recv.at[3 + i], peers(*here, "first", step))
        copy.start()
        twos.append(copy)
    sibling = peers(*here, "core", 1)
    threes = [remote(whole, whole, send.at[6], recv.at[6], sibling)]
    threes[0].start()
    for i, step in ((1, 1), (2, 3), (0, 2)):
        twos[i].wait_recv()
        block = at(base, lax.rem(first + 4 - step, 4), 32)
        copy = remote(block, block, send.at[7 + i], recv.at[7 + i], sibling)
        copy.start()
        threes.append(copy)
    for copy in threes:
        copy.wait_recv()
    for copy in copies + twos + threes:
        copy.wait_send()


def reduce_probe(pg, probe):
    vmem = pl.BlockSpec(memory_space=VMEM)
    return pl.pallas_call(
        reduce_kernel,
        in_specs=[vmem, vmem],
        out_specs=vmem,
        out_shape=jax.ShapeDtypeStruct((2 * MODES, 8, SIDE), f32),
        scratch_shapes=[
            pltpu.VMEM((PLANES, HALF, SIDE), f32),
            pltpu.VMEM((PLANES, HALF, SIDE), f32),
            pltpu.VMEM((3, PLANES, 32, SIDE), f32),
            pltpu.VMEM((3, PLANES, 8, SIDE), f32),
            pltpu.VMEM((4, PLANES, 8, SIDE), f32),
            pltpu.SemaphoreType.DMA((13,)),
            pltpu.SemaphoreType.DMA((13,)),
        ],
        compiler_params=pltpu.CompilerParams(
            collective_id=0, has_side_effects=True, vmem_limit_bytes=24 * 2**20
        ),
        name="reduce_probe",
    )(pg, probe)


def spread_probe(shard):
    vmem = pl.BlockSpec(memory_space=VMEM)
    return pl.pallas_call(
        spread_kernel,
        in_specs=[vmem],
        out_specs=vmem,
        out_shape=jax.ShapeDtypeStruct((2 * MODES, SIDE, SIDE), f32),
        scratch_shapes=[pltpu.SemaphoreType.DMA((10,)), pltpu.SemaphoreType.DMA((10,))],
        compiler_params=pltpu.CompilerParams(
            collective_id=1, has_side_effects=True, vmem_limit_bytes=24 * 2**20
        ),
        name="spread_probe",
    )(shard)


def shards(object_field, probe_modes, offsets, live_counts, patterns):
    tile_rows, tile_cols = object_field.shape[1:]
    chunks = tile_cols // SIDE
    batches, capacity = offsets.shape[:2]
    mats = jnp.asarray(matrices())
    anchor = jnp.stack([lax.axis_index("row") * tile_rows, lax.axis_index("col") * tile_cols])
    local = offsets - anchor[None, None, :]
    row_at, col_at = local[..., 0], local[..., 1]
    live = (jnp.arange(capacity)[None, :] < live_counts).astype(jnp.int32)
    own = jnp.stack([col_at // SIDE, row_at, col_at % SIDE, live], axis=-1)
    two = jnp.stack([own, shifted(own, "row", 1)], axis=1)
    infos = jnp.concatenate([two, shifted(two, "col", 1)], axis=1)
    ordered = [order_patterns(patterns[b]) for b in range(batches)]

    tile, probe = object_field, probe_modes
    rim = shifted(tile[:, :, :SIDE], "col", -1)
    for b in range(batches):
        info = infos[b]
        below = [shifted(pack(info[1, s], tile, rim), "row", -1) for s in range(capacity)]
        base, weight = prepare(info, tile, rim, probe)
        if b + 1 < batches:
            side = jnp.concatenate([base[:, :, :SIDE], weight[:1]], axis=0)
            side = shifted(side, "col", -1)
        pg, own_grads, arrived = None, [], []
        for s in range(capacity):
            grad, pg = run_slot(info[0, s], s, tile, rim, below[s], ordered[b], probe, mats, pg)
            own_grads.append(grad)
            arrived.append(shifted(grad, "row", 1))
        acc = gather(info, own_grads, arrived, chunks)
        from_left = shifted(acc[chunks], "col", 1)
        if b + 1 < batches:
            from_right = shifted(acc[0], "col", -1)
            rim = side[:2] - step_object * (acc[chunks] + from_right) / (side[2] + object_floor)
        tile = update(base, acc, weight, from_left)
        shard = reduce_probe(pg, probe.reshape(2 * MODES, SIDE, SIDE))
        probe = spread_probe(shard).reshape(probe.shape)
    return (tile, probe)


def solution(mesh):
    placed = (
        P(None, "row", "col"),
        P(),
        P(None, ("row", "col"), None),
        P(None, ("row", "col")),
        P(None, ("row", "col"), None, None),
    )
    return jax.shard_map(
        shards, mesh=mesh, in_specs=placed, out_specs=(P(None, "row", "col"), P()), check_vma=False
    )
```

```python
import functools
import math

import jax
import jax.numpy as jnp
import ml_dtypes
import numpy as np
from jax import lax
from jax.experimental import pallas as pl
from jax.experimental.pallas import tpu as pltpu
from jax.sharding import PartitionSpec as P

step_object = 1.0
step_probe = 1.0
smoothing = 0.05
object_floor = 1.0
probe_floor = 0.001
SIDE = 256
HALF = 128
MODES = 4
VMEM = pltpu.VMEM
f32 = jnp.float32


def shifted(value, axis, steps):
    count = lax.axis_size(axis)
    leading, last = (max(0, -steps), min(count, count - steps))
    return lax.ppermute(value, axis, [(source, source + steps) for source in range(leading, last)])


def matrices():
    k, n = np.arange(HALF)[:, None], np.arange(HALF)[None, :]
    out = []
    for odd in (0, 1):
        angle = -2.0 * np.pi * (((2 * k + odd) * n) % SIDE) / SIDE
        re, im = np.cos(angle) / math.sqrt(SIDE), np.sin(angle) / math.sqrt(SIDE)
        big = np.block([[re, -im], [im, re]])
        for matrix in (big, big.T):
            high = matrix.astype(ml_dtypes.bfloat16)
            low = (matrix - high.astype(np.float64)).astype(ml_dtypes.bfloat16)
            out += [high, low]
    return np.stack(out)


def split(value):
    high = value.astype(jnp.bfloat16)
    return high, (value - high.astype(f32)).astype(jnp.bfloat16)


def dot(a, b):
    return jnp.dot(a, b, preferred_element_type=f32)


def left(mats, index, value):
    high, low = split(value)
    a, b = mats[index], mats[index + 1]
    return dot(a, high) + dot(b, high) + dot(a, low)


def right(value, mats, index):
    high, low = split(value)
    a, b = mats[index], mats[index + 1]
    return dot(high, a) + dot(high, b) + dot(low, a)


def cat(axis, *values):
    return jnp.concatenate(values, axis=axis)


def iotas():
    shape = (SIDE, SIDE)
    return lax.broadcasted_iota(jnp.int32, shape, 0), lax.broadcasted_iota(jnp.int32, shape, 1)


def roll2(value, rows, cols):
    return pltpu.roll(pltpu.roll(value, rows, 0), cols, 1)


MESH = pl.DeviceIdType.MESH
PLANES = 2 * MODES + 1


def at(base, index, size):
    return pl.ds(pl.multiple_of(base + index * size, 8), size)


class Links:
    def __init__(self, send, recv):
        self.send, self.recv, self.used = send, recv, 0

    def copy(self, src, dst, device_id):
        i = self.used
        self.used += 1
        made = pltpu.make_async_remote_copy(
            src_ref=src,
            dst_ref=dst,
            send_sem=self.send.at[i],
            recv_sem=self.recv.at[i],
            device_id=device_id,
            device_id_type=MESH,
        )
        made.start()
        return made


def whole_kernel(
    batches, slots, chunks, mesh_rows, mesh_cols,
    info, tile, probe_in, pats_in, mats, perm, out_tile, out_probe,
    ext, probe, raw, pats, rolled, arrived, grads, gained, acc, base, weight, side, from_left, from_right,
    above, below, before, psi, pg, got1, half, got2, got3, got4, send, recv, slot_send, slot_recv, local,
):
    row, col = lax.axis_index("row"), lax.axis_index("col")
    y, x, z, core = lax.div(row, 4), lax.rem(row, 4), lax.div(col, 2), lax.rem(col, 2)
    first, second = y + core * (z - y), z + core * (y - z)
    device = lambda y, x, z, core: (y * 4 + x, z * 2 + core)
    sibling = device(y, x, z, 1 - core)
    turn = lambda value, step: lax.rem(value + step, 4)
    along_first = lambda j: device(turn(y, j * (1 - core)), x, turn(z, j * core), core)
    along_second = lambda j: device(turn(y, j * core), x, turn(z, j * (1 - core)), core)
    along_x = lambda j: device(y, turn(x, j), z, core)
    up = (lax.rem(row + mesh_rows - 1, mesh_rows), col)
    down = (lax.rem(row + 1, mesh_rows), col)
    before_me = (row, lax.rem(col + mesh_cols - 1, mesh_cols))
    after_me = (row, lax.rem(col + 1, mesh_cols))
    links = Links(send, recv)

    loads = [
        pltpu.make_async_copy(tile.at[:, :, pl.ds(j * SIDE, SIDE)], ext.at[j], local.at[j])
        for j in range(chunks)
    ]
    loads.append(pltpu.make_async_copy(pats_in, raw, local.at[chunks]))
    loads.append(pltpu.make_async_copy(probe_in, probe.at[0], local.at[chunks + 1]))
    for load in loads:
        load.start()
    barrier = pltpu.get_barrier_semaphore()
    peers = [sibling, up, down, before_me, after_me]
    peers += [f(j) for f in (along_first, along_second, along_x) for j in (1, 2, 3)]
    for peer in peers:
        pl.semaphore_signal(barrier, inc=1, device_id=peer, device_id_type=MESH)
    pl.semaphore_wait(barrier, len(peers))

    rows, cols = iotas()
    rim = links.copy(tile.at[:, :, pl.ds(0, SIDE)], ext.at[chunks], before_me)
    sent = [rim]

    def where_to(b, who, s, rows_below):
        k, r, cm, live = [info[b, who, s, j] for j in range(4)]
        inside = (rows < r) if rows_below else (rows >= r)
        return jnp.where(inside & (live == 1), k + (cols < cm).astype(jnp.int32), -1)

    def start_halos(b):
        return [
            links.copy(ext.at[pl.ds(0, chunks), :, pl.ds(SIDE - 8, 8), :], above.at[b], down),
            links.copy(ext.at[pl.ds(0, chunks), :, pl.ds(0, 8), :], below.at[b], up),
            links.copy(ext.at[chunks - 1, :, :, pl.ds(HALF, HALF)], before.at[b], after_me),
        ]

    def slot_copy(b, s, kind):
        src, dst, peer = (rolled, arrived, up) if kind == 0 else (grads, gained, down)
        i = (2 * b + kind) * slots + s
        return pltpu.make_async_remote_copy(
            src_ref=src.at[s],
            dst_ref=dst.at[b, s],
            send_sem=slot_send.at[i],
            recv_sem=slot_recv.at[i],
            device_id=peer,
            device_id_type=MESH,
        )

    def start_rims(b):
        def one(s, carry):
            k, cm = info[b, 1, s, 0], info[b, 1, s, 2]
            for part in range(2):
                rolled[s, part] = jnp.where(cols >= cm, ext[k, part], ext[k + 1, part])
            slot_copy(b, s, 0).start()
            return carry

        lax.fori_loop(0, slots, one, 0)

    def order_patterns():
        def one(i, carry):
            high, low = split(raw[i])
            value = dot(perm[0], high) + dot(perm[0], low)
            high, low = split(value)
            pats[i] = dot(high, perm[1]) + dot(low, perm[1])
            return carry

        lax.fori_loop(0, batches * slots, one, 0)

    def prepare(b, halos):
        power = probe[b, 0] * probe[b, 0]
        for plane in range(1, 2 * MODES):
            power = power + probe[b, plane] * probe[b, plane]
        pg[2 * MODES] = power
        weight[...] = jnp.zeros_like(weight)

        def one(s, carry):
            for who in range(4):
                value = roll2(pg[2 * MODES], info[b, who, s, 1], info[b, who, s, 2])
                chunk = where_to(b, who, s, who % 2 == 1)
                if who < 2:
                    for j in range(chunks):
                        weight[j] += jnp.where(chunk == j, value, 0.0)
                else:
                    weight[0] += jnp.where(chunk == chunks, value, 0.0)
            return carry

        lax.fori_loop(0, slots, one, 0)
        for copy in halos:
            copy.wait_recv()
        for part in range(2):
            for j in range(chunks):
                here = ext[j, part]
                top = jnp.where(row > 0, above[b, j, part, 7:8, :], 0.0)
                bottom = jnp.where(row < mesh_rows - 1, below[b, j, part, 0:1, :], 0.0)
                if j > 0:
                    lhs = ext[j - 1, part, :, HALF:][:, HALF - 1 : HALF]
                else:
                    lhs = jnp.where(col > 0, before[b, part, :, HALF - 1 : HALF], 0.0)
                rhs = ext[j + 1, part, :, :HALF][:, 0:1]
                if j == chunks - 1:
                    rhs = jnp.where(col < mesh_cols - 1, rhs, 0.0)
                neighbours = jnp.where(rows == 0, top, pltpu.roll(here, 1, 0))
                neighbours += jnp.where(rows == SIDE - 1, bottom, pltpu.roll(here, SIDE - 1, 0))
                neighbours += jnp.where(cols == 0, lhs, pltpu.roll(here, 1, 1))
                neighbours += jnp.where(cols == SIDE - 1, rhs, pltpu.roll(here, SIDE - 1, 1))
                base[j, part] = here + (step_object * smoothing) * (neighbours - 4.0 * here)
        if b + 1 < batches:
            copies = [
                links.copy(base.at[0], side.at[pl.ds(0, 2)], before_me),
                links.copy(weight.at[0], side.at[2], before_me),
            ]
            sent.extend(copies)
            return copies
        return []

    def run_slots(b):
        pg[...] = jnp.zeros_like(pg)

        def one(s, carry):
            slot_copy(b, s, 0).wait_recv()
            k, r, cm, live = [info[b, 0, s, j] for j in range(4)]
            alive = live.astype(f32)
            window = []
            for part in range(2):
                own = jnp.where(cols >= cm, ext[k, part], ext[k + 1, part])
                value = jnp.where(rows >= r, own, arrived[b, s, part])
                window.append(roll2(value, lax.rem(SIDE - r, SIDE), lax.rem(SIDE - cm, SIDE)))
            xr, xi = window
            total_e = total_o = None
            for m in range(MODES):
                pr, pi = probe[b, 2 * m], probe[b, 2 * m + 1]
                wr, wi = pr * xr - pi * xi, pr * xi + pi * xr
                even = left(mats, 0, cat(0, wr[:HALF] + wr[HALF:], wi[:HALF] + wi[HALF:]))
                odd = left(mats, 4, cat(0, wr[:HALF] - wr[HALF:], wi[:HALF] - wi[HALF:]))
                tr, ti = cat(0, even[:HALF], odd[:HALF]), cat(0, even[HALF:], odd[HALF:])
                pe = right(cat(1, tr[:, :HALF] + tr[:, HALF:], ti[:, :HALF] + ti[:, HALF:]), mats, 2)
                po = right(cat(1, tr[:, :HALF] - tr[:, HALF:], ti[:, :HALF] - ti[:, HALF:]), mats, 6)
                psi[m, 0], psi[m, 1] = pe, po
                total_e = pe * pe if m == 0 else total_e + pe * pe
                total_o = po * po if m == 0 else total_o + po * po
            pattern = pats[b * slots + s]
            de = (total_e[:, :HALF] + total_e[:, HALF:] - pattern[:, :HALF]) * alive
            do = (total_o[:, :HALF] + total_o[:, HALF:] - pattern[:, HALF:]) * alive
            de, do = cat(1, de, de), cat(1, do, do)
            grad_r = grad_i = None
            for m in range(MODES):
                ue, uo = right(psi[m, 0] * de, mats, 0), right(psi[m, 1] * do, mats, 4)
                plus, minus = ue + uo, ue - uo
                tr, ti = cat(1, plus[:, :HALF], minus[:, :HALF]), cat(1, plus[:, HALF:], minus[:, HALF:])
                ze = left(mats, 2, cat(0, tr[:HALF], ti[:HALF]))
                zo = left(mats, 6, cat(0, tr[HALF:], ti[HALF:]))
                plus, minus = ze + zo, ze - zo
                br, bi = cat(0, plus[:HALF], minus[:HALF]), cat(0, plus[HALF:], minus[HALF:])
                pr, pi = probe[b, 2 * m], probe[b, 2 * m + 1]
                gr, gi = pr * br + pi * bi, pr * bi - pi * br
                grad_r = gr if m == 0 else grad_r + gr
                grad_i = gi if m == 0 else grad_i + gi
                pg[2 * m] += xr * br + xi * bi
                pg[2 * m + 1] += xr * bi - xi * br
            pg[2 * MODES] += (xr * xr + xi * xi) * alive
            grads[s, 0] = roll2(grad_r, r, cm)
            grads[s, 1] = roll2(grad_i, r, cm)
            slot_copy(b, s, 1).start()
            return carry

        lax.fori_loop(0, slots, one, 0)

    def gather(b, s):
        slot_copy(b, s, 1).wait_recv()
        own, theirs = where_to(b, 0, s, False), where_to(b, 1, s, True)
        for part in range(2):
            for j in range(chunks + 1):
                value = jnp.where(own == j, grads[s, part], 0.0) + jnp.where(theirs == j, gained[b, s, part], 0.0)
                if s == 0:
                    acc[j, part] = value
                else:
                    acc[j, part] += value

    order = (2, 1, 3, 0)

    def reduce_cores():
        ones = []
        for step in order:
            theirs, there = at((1 - core) * HALF, turn(second, step), 32), at(0, turn(second, step), 32)
            ones.append(links.copy(pg.at[:, theirs, :], got1.at[:, there, :], sibling))
        sent.extend(ones)
        return ones

    def reduce_first(ones):
        twos = []
        for i, step in enumerate(order):
            piece = turn(first, step)
            ones[i].wait_recv()
            mine, there = at(core * HALF, piece, 32), at(0, piece, 32)
            half[:, there, :] = pg[:, mine, :] + got1[:, there, :]
            if step:
                twos.append(links.copy(half.at[:, there, :], got2.at[step - 1], along_first(step)))
        sent.extend(twos)
        return twos

    def reduce_second(twos):
        threes = []
        for copy in twos:
            copy.wait_recv()
        for step in order:
            piece = turn(second, step)
            there, within = at(first * 32, piece, 8), at(0, piece, 8)
            value = half[:, there, :] + got2[0, :, within, :]
            half[:, there, :] = value + got2[1, :, within, :] + got2[2, :, within, :]
            if step:
                threes.append(links.copy(half.at[:, there, :], got3.at[step - 1], along_second(step)))
        sent.extend(threes)
        return threes

    def reduce_x(threes):
        fours = []
        for copy in threes:
            copy.wait_recv()
        there = at(first * 32, second, 8)
        got4[x] = half[:, there, :] + got3[0] + got3[1] + got3[2]
        for step in (2, 1, 3):
            fours.append(links.copy(got4.at[x], got4.at[x], along_x(step)))
        sent.extend(fours)
        return fours

    def spread_second(b, fours):
        for copy in fours:
            copy.wait_recv()
        total = got4[0] + got4[1] + got4[2] + got4[3]
        scale = step_probe / (total[2 * MODES] + probe_floor)
        mine = at(core * HALF + first * 32, second, 8)
        new = probe.at[b + 1]
        for plane in range(2 * MODES):
            new[plane, mine, :] = probe[b, plane, mine, :] - scale * total[plane]
        block = new.at[:, mine, :]
        copies = [links.copy(block, block, along_second(step)) for step in (2, 1, 3)]
        sent.extend(copies)
        return copies

    def spread_first(b, copies):
        for copy in copies:
            copy.wait_recv()
        block = probe.at[b + 1, :, at(core * HALF, first, 32), :]
        twos = [links.copy(block, block, along_first(step)) for step in (2, 1, 3)]
        threes = [links.copy(block, block, sibling)]
        sent.extend(twos + threes)
        return twos, threes

    def spread_cores(b, twos, threes):
        for i, step in ((1, 1), (2, 3), (0, 2)):
            twos[i].wait_recv()
            block = probe.at[b + 1, :, at(core * HALF, turn(first, 4 - step), 32), :]
            copy = links.copy(block, block, sibling)
            threes.append(copy)
            sent.append(copy)
        for copy in threes:
            copy.wait_recv()

    for load in loads[:chunks]:
        load.wait()
    halos = start_halos(0)
    for load in loads[chunks:]:
        load.wait()
    order_patterns()
    rim.wait_recv()
    start_rims(0)
    got1s, got2s, got3s, got4s = got1, got2, got3, got4
    stores = []
    for b in range(batches):
        more = b + 1 < batches
        got1, got2, got3, got4 = got1s.at[b], got2s.at[b], got3s.at[b], got4s.at[b]
        sides = prepare(b, halos)
        run_slots(b)
        ones = reduce_cores()
        for s in range(slots - 1):
            gather(b, s)
        twos = reduce_first(ones)
        gather(b, slots - 1)
        to_right = links.copy(acc.at[chunks], from_left.at[b], after_me)
        sent.append(to_right)
        if more:
            to_left = links.copy(acc.at[0], from_right, before_me)
            sent.append(to_left)
        threes = reduce_second(twos)
        fours = reduce_x(threes)
        if not more:
            spread = spread_second(b, fours)
        for copy in halos:
            copy.wait_send()
        for j in list(range(1, chunks)) + [0]:
            if j == 0:
                to_right.wait_recv()
            scale = step_object / (weight[j] + object_floor)
            for part in range(2):
                value = acc[j, part] + from_left[b, part] if j == 0 else acc[j, part]
                ext[j, part] = base[j, part] - scale * value
            if not more:
                store = pltpu.make_async_copy(ext.at[j], out_tile.at[:, :, pl.ds(j * SIDE, SIDE)], local.at[j])
                store.start()
                stores.append(store)
        for s in range(slots):
            slot_copy(b, s, 0).wait_send()
            slot_copy(b, s, 1).wait_send()
        if more:
            to_left.wait_recv()
            for copy in sides:
                copy.wait_recv()
            scale = step_object / (side[2] + object_floor)
            for part in range(2):
                ext[chunks, part] = side[part] - scale * (acc[chunks, part] + from_right[part])
            start_rims(b + 1)
            halos = start_halos(b + 1)
            spread = spread_second(b, fours)
        twos, threes = spread_first(b, spread)
        spread_cores(b, twos, threes)
        if more:
            for copy in sent:
                copy.wait_send()
            sent.clear()
    last = pltpu.make_async_copy(probe.at[batches], out_probe, local.at[chunks + 1])
    last.start()
    for copy in sent:
        copy.wait_send()
    for store in stores + [last]:
        store.wait()


def shards(object_field, probe_modes, offsets, live_counts, patterns):
    tile_rows, tile_cols = object_field.shape[1:]
    chunks = tile_cols // SIDE
    batches, slots = offsets.shape[:2]
    mesh_rows, mesh_cols = lax.axis_size("row"), lax.axis_size("col")
    anchor = jnp.stack([lax.axis_index("row") * tile_rows, lax.axis_index("col") * tile_cols])
    local = offsets - anchor[None, None, :]
    row_at, col_at = local[..., 0], local[..., 1]
    live = (jnp.arange(slots)[None, :] < live_counts).astype(jnp.int32)
    own = jnp.stack([col_at // SIDE, row_at, col_at % SIDE, live], axis=-1)
    two = jnp.stack([own, shifted(own, "row", 1)], axis=1)
    info = jnp.concatenate([two, shifted(two, "col", 1)], axis=1)
    perm = np.zeros((SIDE, SIDE), np.float32)
    j = np.arange(SIDE)
    perm[j, (j % 2) * HALF + j // 2] = 1.0
    perm = jnp.asarray(np.stack([perm.T, perm]), jnp.bfloat16)

    vmem, hbm = pl.BlockSpec(memory_space=VMEM), pl.BlockSpec(memory_space=pl.ANY)
    block = (2, SIDE, SIDE)
    buf = lambda *shape: pltpu.VMEM(shape, f32)
    dma = pltpu.SemaphoreType.DMA
    tile, probe = pl.pallas_call(
        functools.partial(whole_kernel, batches, slots, chunks, mesh_rows, mesh_cols),
        in_specs=[pl.BlockSpec(memory_space=pltpu.SMEM), hbm, hbm, hbm, vmem, vmem],
        out_specs=[hbm, hbm],
        out_shape=[
            jax.ShapeDtypeStruct(object_field.shape, f32),
            jax.ShapeDtypeStruct((2 * MODES, SIDE, SIDE), f32),
        ],
        scratch_shapes=[
            buf(chunks + 1, *block),
            buf(batches + 1, 2 * MODES, SIDE, SIDE),
            buf(batches * slots, SIDE, SIDE),
            buf(batches * slots, SIDE, SIDE),
            buf(slots, *block),
            buf(batches, slots, *block),
            buf(slots, *block),
            buf(batches, slots, *block),
            buf(chunks + 1, *block),
            buf(chunks, *block),
            buf(chunks, SIDE, SIDE),
            buf(3, SIDE, SIDE),
            buf(batches, *block),
            buf(*block),
            buf(batches, chunks, 2, 8, SIDE),
            buf(batches, chunks, 2, 8, SIDE),
            buf(batches, 2, SIDE, HALF),
            buf(MODES, *block),
            buf(PLANES, SIDE, SIDE),
            buf(batches, PLANES, HALF, SIDE),
            buf(PLANES, HALF, SIDE),
            buf(batches, 3, PLANES, 32, SIDE),
            buf(batches, 3, PLANES, 8, SIDE),
            buf(batches, 4, PLANES, 8, SIDE),
            dma((80,)),
            dma((80,)),
            dma((2 * batches * slots,)),
            dma((2 * batches * slots,)),
            dma((chunks + 2,)),
        ],
        compiler_params=pltpu.CompilerParams(
            collective_id=0, has_side_effects=True, vmem_limit_bytes=60 * 2**20
        ),
        name="reconstruct",
    )(
        info,
        object_field,
        probe_modes.reshape(2 * MODES, SIDE, SIDE),
        patterns.reshape(batches * slots, SIDE, SIDE),
        jnp.asarray(matrices()),
        perm,
    )
    return (tile, probe.reshape(probe_modes.shape))


def solution(mesh):
    placed = (
        P(None, "row", "col"),
        P(),
        P(None, ("row", "col"), None),
        P(None, ("row", "col")),
        P(None, ("row", "col"), None, None),
    )
    return jax.shard_map(
        shards, mesh=mesh, in_specs=placed, out_specs=(P(None, "row", "col"), P()), check_vma=False
    )
```

```python
import functools
import math

import jax
import jax.numpy as jnp
import ml_dtypes
import numpy as np
from jax import lax
from jax.experimental import pallas as pl
from jax.experimental.pallas import tpu as pltpu
from jax.sharding import PartitionSpec as P

step_object = 1.0
step_probe = 1.0
smoothing = 0.05
object_floor = 1.0
probe_floor = 0.001
SIDE = 256
HALF = 128
MODES = 4
VMEM = pltpu.VMEM
f32 = jnp.float32


def matrices():
    k, n = np.arange(HALF)[:, None], np.arange(HALF)[None, :]
    out = []
    for odd in (0, 1):
        angle = -2.0 * np.pi * (((2 * k + odd) * n) % SIDE) / SIDE
        re, im = np.cos(angle) / math.sqrt(SIDE), np.sin(angle) / math.sqrt(SIDE)
        big = np.block([[re, -im], [im, re]])
        for matrix in (big, big.T):
            high = matrix.astype(ml_dtypes.bfloat16)
            low = (matrix - high.astype(np.float64)).astype(ml_dtypes.bfloat16)
            out += [high, low]
    return np.stack(out)


def split(value):
    high = value.astype(jnp.bfloat16)
    return high, (value - high.astype(f32)).astype(jnp.bfloat16)


def dot(a, b):
    return jnp.dot(a, b, preferred_element_type=f32)


def left(mats, index, value):
    high, low = split(value)
    a, b = mats[index], mats[index + 1]
    return dot(a, high) + dot(b, high) + dot(a, low)


def right(value, mats, index):
    high, low = split(value)
    a, b = mats[index], mats[index + 1]
    return dot(high, a) + dot(high, b) + dot(low, a)


def cat(axis, *values):
    return jnp.concatenate(values, axis=axis)


def iotas():
    shape = (SIDE, SIDE)
    return lax.broadcasted_iota(jnp.int32, shape, 0), lax.broadcasted_iota(jnp.int32, shape, 1)


def roll2(value, rows, cols):
    return pltpu.roll(pltpu.roll(value, rows, 0), cols, 1)


MESH = pl.DeviceIdType.MESH
PLANES = 2 * MODES + 1


def at(base, index, size):
    return pl.ds(pl.multiple_of(base + index * size, 8), size)


class Links:
    def __init__(self, send, recv):
        self.send, self.recv, self.used = send, recv, 0

    def copy(self, src, dst, device_id):
        i = self.used
        self.used += 1
        made = pltpu.make_async_remote_copy(
            src_ref=src,
            dst_ref=dst,
            send_sem=self.send.at[i],
            recv_sem=self.recv.at[i],
            device_id=device_id,
            device_id_type=MESH,
        )
        made.start()
        return made


def whole_kernel(
    batches, slots, chunks, mesh_rows, mesh_cols,
    spots, tile, probe_in, pats_in, mats, perm, out_tile, out_probe, theirs_info,
    ext, probe, raw, pats, rolled, arrived, grads, gained, acc, base, weight, side, from_left, from_right,
    above, below, before, psi, pg, got1, half, relay, got2, got3, got4, send, recv, slot_send, slot_recv, local,
):
    row, col = lax.axis_index("row"), lax.axis_index("col")
    y, x, z, core = lax.div(row, 4), lax.rem(row, 4), lax.div(col, 2), lax.rem(col, 2)
    first, second = y + core * (z - y), z + core * (y - z)
    device = lambda y, x, z, core: (y * 4 + x, z * 2 + core)
    sibling = device(y, x, z, 1 - core)
    turn = lambda value, step: lax.rem(value + step, 4)
    along_first = lambda j: device(turn(y, j * (1 - core)), x, turn(z, j * core), core)
    along_second = lambda j: device(turn(y, j * core), x, turn(z, j * (1 - core)), core)
    along_x = lambda j: device(y, turn(x, j), z, core)
    up = (lax.rem(row + mesh_rows - 1, mesh_rows), col)
    down = (lax.rem(row + 1, mesh_rows), col)
    before_me = (row, lax.rem(col + mesh_cols - 1, mesh_cols))
    after_me = (row, lax.rem(col + 1, mesh_cols))
    down_right = (down[0], after_me[1])
    up_left = (up[0], before_me[1])
    links = Links(send, recv)

    loads = [
        pltpu.make_async_copy(tile.at[:, :, pl.ds(j * SIDE, SIDE)], ext.at[j], local.at[j])
        for j in range(chunks)
    ]
    kept = slots - 1
    for b in range(batches):
        mine = pl.ds(b * slots, kept)
        loads.append(pltpu.make_async_copy(pats_in.at[mine], raw.at[mine], local.at[chunks + 2 + b]))
    loads.append(pltpu.make_async_copy(probe_in, probe.at[0], local.at[chunks + 1]))
    for load in loads:
        load.start()
    barrier = pltpu.get_barrier_semaphore()
    peers = [sibling, up, down, before_me, after_me, down_right, up_left]
    peers += [f(j) for f in (along_first, along_second, along_x) for j in (1, 2, 3)]
    for peer in peers:
        pl.semaphore_signal(barrier, inc=1, device_id=peer, device_id_type=MESH)
    pl.semaphore_wait(barrier, len(peers))

    rows, cols = iotas()
    infos = [
        links.copy(spots, theirs_info.at[i], peer) for i, peer in enumerate((down, after_me, down_right))
    ]
    rim = links.copy(tile.at[:, :, pl.ds(0, SIDE)], ext.at[chunks], before_me)
    handed = [
        links.copy(pats_in.at[b * slots + kept], raw.at[b * slots + kept], down) for b in range(batches)
    ]
    sent = infos + [rim] + handed

    def spot(b, who, s):
        read = (lambda i: spots[i]) if who == 0 else (lambda i: theirs_info[who - 1, i])
        r = lax.rem(read(2 * (b * slots + s)), SIDE)
        c = lax.rem(read(2 * (b * slots + s) + 1), SIDE * chunks)
        live = (s < read(2 * batches * slots + b)) * 1
        return lax.div(c, SIDE), r, lax.rem(c, SIDE), live

    def where_to(b, who, s, rows_below):
        k, r, cm, live = spot(b, who, s)
        inside = (rows < r) if rows_below else (rows >= r)
        return jnp.where(inside & (live == 1), k + (cols < cm).astype(jnp.int32), -1)

    def start_halos(b):
        return [
            links.copy(ext.at[pl.ds(0, chunks), :, pl.ds(SIDE - 8, 8), :], above.at[b], down),
            links.copy(ext.at[pl.ds(0, chunks), :, pl.ds(0, 8), :], below.at[b], up),
            links.copy(ext.at[chunks - 1, :, :, pl.ds(HALF, HALF)], before.at[b], after_me),
        ]

    def slot_copy(b, s, kind, away):
        src, dst = (rolled, arrived) if kind == 0 else (grads, gained)
        step = (1 - away) * (mesh_rows - 2) if kind == 0 else away * (mesh_rows - 2)
        i = (2 * b + kind) * slots + s
        return pltpu.make_async_remote_copy(
            src_ref=src.at[s],
            dst_ref=dst.at[b, s],
            send_sem=slot_send.at[i],
            recv_sem=slot_recv.at[i],
            device_id=(lax.rem(row + 1 + step, mesh_rows), col),
            device_id_type=MESH,
        )

    def start_rim(b, s):
        away = int(s == kept)
        k, r, cm, live = spot(b, 1 - away, s)
        for part in range(2):
            rolled[s, part] = jnp.where(cols >= cm, ext[k, part], ext[k + 1, part])
        slot_copy(b, s, 0, away).start()

    def order_patterns(b):
        def one(i, carry):
            high, low = split(raw[i])
            value = dot(perm[0], high) + dot(perm[0], low)
            high, low = split(value)
            pats[i] = dot(high, perm[1]) + dot(low, perm[1])
            return carry

        lax.fori_loop(b * slots, (b + 1) * slots, one, 0)

    def prepare(b, halos):
        power = probe[b, 0] * probe[b, 0]
        for plane in range(1, 2 * MODES):
            power = power + probe[b, plane] * probe[b, plane]
        pg[2 * MODES] = power
        weight[...] = jnp.zeros_like(weight)

        def one(s, carry):
            for who in range(4):
                value = roll2(pg[2 * MODES], *spot(b, who, s)[1:3])
                chunk = where_to(b, who, s, who % 2 == 1)
                if who < 2:
                    for j in range(chunks):
                        weight[j] += jnp.where(chunk == j, value, 0.0)
                else:
                    weight[0] += jnp.where(chunk == chunks, value, 0.0)
            return carry

        lax.fori_loop(0, slots, one, 0)
        for copy in halos:
            copy.wait_recv()
        for part in range(2):
            for j in range(chunks):
                here = ext[j, part]
                top = jnp.where(row > 0, above[b, j, part, 7:8, :], 0.0)
                bottom = jnp.where(row < mesh_rows - 1, below[b, j, part, 0:1, :], 0.0)
                if j > 0:
                    lhs = ext[j - 1, part, :, HALF:][:, HALF - 1 : HALF]
                else:
                    lhs = jnp.where(col > 0, before[b, part, :, HALF - 1 : HALF], 0.0)
                rhs = ext[j + 1, part, :, :HALF][:, 0:1]
                if j == chunks - 1:
                    rhs = jnp.where(col < mesh_cols - 1, rhs, 0.0)
                neighbours = jnp.where(rows == 0, top, pltpu.roll(here, 1, 0))
                neighbours += jnp.where(rows == SIDE - 1, bottom, pltpu.roll(here, SIDE - 1, 0))
                neighbours += jnp.where(cols == 0, lhs, pltpu.roll(here, 1, 1))
                neighbours += jnp.where(cols == SIDE - 1, rhs, pltpu.roll(here, SIDE - 1, 1))
                base[j, part] = here + (step_object * smoothing) * (neighbours - 4.0 * here)
        if b + 1 < batches:
            copies = [
                links.copy(base.at[0], side.at[pl.ds(0, 2)], before_me),
                links.copy(weight.at[0], side.at[2], before_me),
            ]
            sent.extend(copies)
            return copies
        return []

    def run_slots(b):
        pg[...] = jnp.zeros_like(pg)

        def one(i, carry):
            s = lax.rem(2 * i, slots)
            away = lax.rem(i, 2)
            slot_copy(b, s, 0, away).wait_recv()
            k, r, cm, live = [jnp.where(away == 1, t, o) for o, t in zip(spot(b, 0, s), spot(b, 1, s))]
            alive = live.astype(f32)
            here = (rows - r) * (1 - 2 * away) - away >= 0
            window = []
            for part in range(2):
                own = jnp.where(cols >= cm, ext[k, part], ext[k + 1, part])
                value = jnp.where(here, own, arrived[b, s, part])
                window.append(roll2(value, lax.rem(SIDE - r, SIDE), lax.rem(SIDE - cm, SIDE)))
            xr, xi = window
            total_e = total_o = None
            for m in range(MODES):
                pr, pi = probe[b, 2 * m], probe[b, 2 * m + 1]
                wr, wi = pr * xr - pi * xi, pr * xi + pi * xr
                even = left(mats, 0, cat(0, wr[:HALF] + wr[HALF:], wi[:HALF] + wi[HALF:]))
                odd = left(mats, 4, cat(0, wr[:HALF] - wr[HALF:], wi[:HALF] - wi[HALF:]))
                tr, ti = cat(0, even[:HALF], odd[:HALF]), cat(0, even[HALF:], odd[HALF:])
                pe = right(cat(1, tr[:, :HALF] + tr[:, HALF:], ti[:, :HALF] + ti[:, HALF:]), mats, 2)
                po = right(cat(1, tr[:, :HALF] - tr[:, HALF:], ti[:, :HALF] - ti[:, HALF:]), mats, 6)
                psi[m, 0], psi[m, 1] = pe, po
                total_e = pe * pe if m == 0 else total_e + pe * pe
                total_o = po * po if m == 0 else total_o + po * po
            pattern = pats[b * slots + s]
            de = (total_e[:, :HALF] + total_e[:, HALF:] - pattern[:, :HALF]) * alive
            do = (total_o[:, :HALF] + total_o[:, HALF:] - pattern[:, HALF:]) * alive
            de, do = cat(1, de, de), cat(1, do, do)
            grad_r = grad_i = None
            for m in range(MODES):
                ue, uo = right(psi[m, 0] * de, mats, 0), right(psi[m, 1] * do, mats, 4)
                plus, minus = ue + uo, ue - uo
                tr, ti = cat(1, plus[:, :HALF], minus[:, :HALF]), cat(1, plus[:, HALF:], minus[:, HALF:])
                ze = left(mats, 2, cat(0, tr[:HALF], ti[:HALF]))
                zo = left(mats, 6, cat(0, tr[HALF:], ti[HALF:]))
                plus, minus = ze + zo, ze - zo
                br, bi = cat(0, plus[:HALF], minus[:HALF]), cat(0, plus[HALF:], minus[HALF:])
                pr, pi = probe[b, 2 * m], probe[b, 2 * m + 1]
                gr, gi = pr * br + pi * bi, pr * bi - pi * br
                grad_r = gr if m == 0 else grad_r + gr
                grad_i = gi if m == 0 else grad_i + gi
                pg[2 * m] += xr * br + xi * bi
                pg[2 * m + 1] += xr * bi - xi * br
            pg[2 * MODES] += (xr * xr + xi * xi) * alive
            grads[s, 0] = roll2(grad_r, r, cm)
            grads[s, 1] = roll2(grad_i, r, cm)
            slot_copy(b, s, 1, away).start()
            return carry

        lax.fori_loop(0, slots, one, 0)

    def gather(b, s):
        away = int(s == kept)
        slot_copy(b, s, 1, away).wait_recv()
        own, theirs = where_to(b, 0, s, False), where_to(b, 1, s, True)
        mine, others = (gained.at[b, s], grads.at[s]) if away else (grads.at[s], gained.at[b, s])
        for part in range(2):
            for j in range(chunks + 1):
                value = jnp.where(own == j, mine[part], 0.0) + jnp.where(theirs == j, others[part], 0.0)
                if s == 0:
                    acc[j, part] = value
                else:
                    acc[j, part] += value

    order = (2, 1, 3, 0)

    def reduce_cores():
        ones = []
        for step in order:
            theirs, there = at((1 - core) * HALF, turn(second, step), 32), at(0, turn(second, step), 32)
            ones.append(links.copy(pg.at[:, theirs, :], got1.at[:, there, :], sibling))
        sent.extend(ones)
        return ones

    def reduce_first(ones):
        def piece(i):
            ones[i].wait_recv()
            index = turn(first, order[i])
            there = at(0, index, 32)
            half[:, there, :] = pg[:, at(core * HALF, index, 32), :] + got1[:, there, :]
            return pl.multiple_of(index * 32, 8)

        far = piece(0)
        rows_of = lambda start, part: pl.ds(pl.multiple_of(start + 16 * part, 8), 16)
        hops = [links.copy(half.at[:, rows_of(far, p), :], relay.at[p], along_first((1, 3)[p])) for p in range(2)]
        near, late = [], []
        for p in range(2):
            start = piece(1 + p)
            rows_now = rows_of(start, 1 - p)
            near.append(
                links.copy(half.at[:, rows_now, :], got2.at[p, :, pl.ds(16 * (1 - p), 16), :], along_first((1, 3)[p]))
            )
            late.append(rows_of(start, p))
        piece(3)
        for p in range(2):
            hops[p].wait_recv()
            half[:, late[p], :] = half[:, late[p], :] + relay[p]
            near.append(
                links.copy(half.at[:, late[p], :], got2.at[p, :, pl.ds(16 * p, 16), :], along_first((1, 3)[p]))
            )
        sent.extend(hops + near)
        return near

    def reduce_second(twos):
        threes = []
        for copy in twos:
            copy.wait_recv()
        for step in order:
            piece = turn(second, step)
            there, within = at(first * 32, piece, 8), at(0, piece, 8)
            half[:, there, :] = half[:, there, :] + got2[0, :, within, :] + got2[1, :, within, :]
            if step:
                threes.append(links.copy(half.at[:, there, :], got3.at[step - 1], along_second(step)))
        sent.extend(threes)
        return threes

    def reduce_x(threes):
        fours = []
        for copy in threes:
            copy.wait_recv()
        there = at(first * 32, second, 8)
        got4[x] = half[:, there, :] + got3[0] + got3[1] + got3[2]
        for step in (2, 1, 3):
            fours.append(links.copy(got4.at[x], got4.at[x], along_x(step)))
        sent.extend(fours)
        return fours

    def spread_second(b, fours):
        for copy in fours:
            copy.wait_recv()
        total = got4[0] + got4[1] + got4[2] + got4[3]
        scale = step_probe / (total[2 * MODES] + probe_floor)
        mine = at(core * HALF + first * 32, second, 8)
        new = probe.at[b + 1]
        for plane in range(2 * MODES):
            new[plane, mine, :] = probe[b, plane, mine, :] - scale * total[plane]
        block = new.at[:, mine, :]
        copies = [links.copy(block, block, along_second(step)) for step in (2, 1, 3)]
        sent.extend(copies)
        return copies

    def spread_first(b, copies):
        for copy in copies:
            copy.wait_recv()
        block = probe.at[b + 1, :, at(core * HALF, first, 32), :]
        twos = [links.copy(block, block, along_first(step)) for step in (1, 3)]
        threes = [links.copy(block, block, sibling)]
        sent.extend(twos + threes)
        return twos, threes

    def spread_cores(b, twos, threes):
        def to(index, start, count, peer):
            there = pl.ds(pl.multiple_of(core * HALF + index * 32 + start, 8), count)
            block = probe.at[b + 1, :, there, :]
            return links.copy(block, block, peer)

        hops = []
        for p in range(2):
            twos[p].wait_recv()
            index = turn(first, (3, 1)[p])
            hops.append(to(index, 16 * p, 16, along_first((1, 3)[p])))
            threes.append(to(index, 0, 32, sibling))
        for p in range(2):
            hops[p].wait_recv()
            threes.append(to(turn(first, 2), 16 * p, 16, sibling))
        for copy in threes:
            copy.wait_recv()
        sent.extend(hops + threes[1:])

    for load in loads[:chunks]:
        load.wait()
    halos = start_halos(0)
    for load in loads[chunks:]:
        load.wait()
    for copy in infos:
        copy.wait_recv()
    rim.wait_recv()
    start_rim(0, 0)
    start_rim(0, kept)
    got1s, got2s, got3s, got4s = got1, got2, got3, got4
    stores = []
    for b in range(batches):
        more = b + 1 < batches
        got1, got2, got3, got4 = got1s.at[b], got2s.at[b], got3s.at[b], got4s.at[b]
        handed[b].wait_recv()
        order_patterns(b)
        sides = prepare(b, halos)
        slot_copy(b, 0, 0, 0).wait_send()
        for s in range(1, kept):
            start_rim(b, s)
        run_slots(b)
        ones = reduce_cores()
        gather(b, 0)
        gather(b, kept)
        twos = reduce_first(ones)
        for s in range(1, kept):
            gather(b, s)
        to_right = links.copy(acc.at[chunks], from_left.at[b], after_me)
        sent.append(to_right)
        if more:
            to_left = links.copy(acc.at[0], from_right, before_me)
            sent.append(to_left)
        threes = reduce_second(twos)
        fours = reduce_x(threes)
        if not more:
            spread = spread_second(b, fours)
        for copy in halos:
            copy.wait_send()
        for j in list(range(1, chunks)) + [0]:
            if j == 0:
                if not more:
                    twos, threes = spread_first(b, spread)
                to_right.wait_recv()
            scale = step_object / (weight[j] + object_floor)
            for part in range(2):
                value = acc[j, part] + from_left[b, part] if j == 0 else acc[j, part]
                ext[j, part] = base[j, part] - scale * value
            if not more:
                store = pltpu.make_async_copy(ext.at[j], out_tile.at[:, :, pl.ds(j * SIDE, SIDE)], local.at[j])
                store.start()
                stores.append(store)
        for s in range(slots):
            away = int(s == kept)
            if s:
                slot_copy(b, s, 0, away).wait_send()
            slot_copy(b, s, 1, away).wait_send()
        if more:
            to_left.wait_recv()
            for copy in sides:
                copy.wait_recv()
            scale = step_object / (side[2] + object_floor)
            for part in range(2):
                ext[chunks, part] = side[part] - scale * (acc[chunks, part] + from_right[part])
            start_rim(b + 1, 0)
            start_rim(b + 1, kept)
            halos = start_halos(b + 1)
            spread = spread_second(b, fours)
            twos, threes = spread_first(b, spread)
        spread_cores(b, twos, threes)
        if more:
            for copy in sent:
                copy.wait_send()
            sent.clear()
    last = pltpu.make_async_copy(probe.at[batches], out_probe, local.at[chunks + 1])
    last.start()
    for copy in sent:
        copy.wait_send()
    for store in stores + [last]:
        store.wait()


def shards(object_field, probe_modes, offsets, live_counts, patterns):
    tile_rows, tile_cols = object_field.shape[1:]
    chunks = tile_cols // SIDE
    batches, slots = offsets.shape[:2]
    mesh_rows, mesh_cols = lax.axis_size("row"), lax.axis_size("col")
    spots = jnp.concatenate([offsets.reshape(-1), live_counts.reshape(-1)])
    spots = jnp.pad(spots, (0, 128 - spots.shape[0]))
    perm = np.zeros((SIDE, SIDE), np.float32)
    j = np.arange(SIDE)
    perm[j, (j % 2) * HALF + j // 2] = 1.0
    perm = jnp.asarray(np.stack([perm.T, perm]), jnp.bfloat16)

    vmem, hbm = pl.BlockSpec(memory_space=VMEM), pl.BlockSpec(memory_space=pl.ANY)
    block = (2, SIDE, SIDE)
    buf = lambda *shape: pltpu.VMEM(shape, f32)
    dma = pltpu.SemaphoreType.DMA
    tile, probe = pl.pallas_call(
        functools.partial(whole_kernel, batches, slots, chunks, mesh_rows, mesh_cols),
        in_specs=[pl.BlockSpec(memory_space=pltpu.SMEM), hbm, hbm, hbm, vmem, vmem],
        out_specs=[hbm, hbm],
        out_shape=[
            jax.ShapeDtypeStruct(object_field.shape, f32),
            jax.ShapeDtypeStruct((2 * MODES, SIDE, SIDE), f32),
        ],
        scratch_shapes=[
            pltpu.SMEM((3, 128), jnp.int32),
            buf(chunks + 1, *block),
            buf(batches + 1, 2 * MODES, SIDE, SIDE),
            buf(batches * slots, SIDE, SIDE),
            buf(batches * slots, SIDE, SIDE),
            buf(slots, *block),
            buf(batches, slots, *block),
            buf(slots, *block),
            buf(batches, slots, *block),
            buf(chunks + 1, *block),
            buf(chunks, *block),
            buf(chunks, SIDE, SIDE),
            buf(3, SIDE, SIDE),
            buf(batches, *block),
            buf(*block),
            buf(batches, chunks, 2, 8, SIDE),
            buf(batches, chunks, 2, 8, SIDE),
            buf(batches, 2, SIDE, HALF),
            buf(MODES, *block),
            buf(PLANES, SIDE, SIDE),
            buf(batches, PLANES, HALF, SIDE),
            buf(PLANES, HALF, SIDE),
            buf(2, PLANES, 16, SIDE),
            buf(batches, 2, PLANES, 32, SIDE),
            buf(batches, 3, PLANES, 8, SIDE),
            buf(batches, 4, PLANES, 8, SIDE),
            dma((100,)),
            dma((100,)),
            dma((2 * batches * slots,)),
            dma((2 * batches * slots,)),
            dma((chunks + 2 + batches,)),
        ],
        compiler_params=pltpu.CompilerParams(
            collective_id=0, has_side_effects=True, vmem_limit_bytes=60 * 2**20
        ),
        name="reconstruct",
    )(
        spots,
        object_field,
        probe_modes.reshape(2 * MODES, SIDE, SIDE),
        patterns.reshape(batches * slots, SIDE, SIDE),
        jnp.asarray(matrices()),
        perm,
    )
    return (tile, probe.reshape(probe_modes.shape))


def solution(mesh):
    placed = (
        P(None, "row", "col"),
        P(),
        P(None, ("row", "col"), None),
        P(None, ("row", "col")),
        P(None, ("row", "col"), None, None),
    )
    return jax.shard_map(
        shards, mesh=mesh, in_specs=placed, out_specs=(P(None, "row", "col"), P()), check_vma=False
    )
```

```python
import functools
import math

import jax
import jax.numpy as jnp
import ml_dtypes
import numpy as np
from jax import lax
from jax.experimental import pallas as pl
from jax.experimental.pallas import tpu as pltpu
from jax.sharding import PartitionSpec as P

step_object = 1.0
step_probe = 1.0
smoothing = 0.05
object_floor = 1.0
probe_floor = 0.001
SIDE = 256
HALF = 128
MODES = 4
VMEM = pltpu.VMEM
f32 = jnp.float32


def matrices():
    k, n = np.arange(HALF)[:, None], np.arange(HALF)[None, :]
    out = []
    for odd in (0, 1):
        angle = -2.0 * np.pi * (((2 * k + odd) * n) % SIDE) / SIDE
        re, im = np.cos(angle) / math.sqrt(SIDE), np.sin(angle) / math.sqrt(SIDE)
        big = np.block([[re, -im], [im, re]])
        for matrix in (big, big.T):
            high = matrix.astype(ml_dtypes.bfloat16)
            low = (matrix - high.astype(np.float64)).astype(ml_dtypes.bfloat16)
            out += [high, low]
    return np.stack(out)


def split(value):
    high = value.astype(jnp.bfloat16)
    return high, (value - high.astype(f32)).astype(jnp.bfloat16)


def dot(a, b):
    return jnp.dot(a, b, preferred_element_type=f32)


def left(mats, index, value):
    high, low = split(value)
    a, b = mats[index], mats[index + 1]
    both = dot(cat(0, a, b), high)
    return both[:SIDE] + both[SIDE:] + dot(a, low)


def right(value, mats, index):
    high, low = split(value)
    a, b = mats[index], mats[index + 1]
    return dot(high, a) + dot(high, b) + dot(low, a)


def cat(axis, *values):
    return jnp.concatenate(values, axis=axis)


def iotas():
    shape = (SIDE, SIDE)
    return lax.broadcasted_iota(jnp.int32, shape, 0), lax.broadcasted_iota(jnp.int32, shape, 1)


def roll2(value, rows, cols):
    return pltpu.roll(pltpu.roll(value, rows, 0), cols, 1)


MESH = pl.DeviceIdType.MESH
PLANES = 2 * MODES + 1


def at(base, index, size):
    return pl.ds(pl.multiple_of(base + index * size, 8), size)


class Links:
    def __init__(self, send, recv):
        self.send, self.recv, self.used = send, recv, 0

    def copy(self, src, dst, device_id):
        i = self.used
        self.used += 1
        made = pltpu.make_async_remote_copy(
            src_ref=src,
            dst_ref=dst,
            send_sem=self.send.at[i],
            recv_sem=self.recv.at[i],
            device_id=device_id,
            device_id_type=MESH,
        )
        made.start()
        return made


def whole_kernel(
    batches, slots, chunks, mesh_rows, mesh_cols,
    spots, tile, probe_in, pats_in, mats, perm, out_tile, out_probe, theirs_info,
    ext, rim_in, probe, raw, pats, rolled, arrived, grads, gained, acc, base, weight, side, from_left, from_right,
    above, below, before, psi, middle, window, total, pg, got1, half, got2, got3, got4, send, recv, slot_send, slot_recv, local,
):
    row, col = lax.axis_index("row"), lax.axis_index("col")
    y, x, z, core = lax.div(row, 4), lax.rem(row, 4), lax.div(col, 2), lax.rem(col, 2)
    first, second = y + core * (z - y), z + core * (y - z)
    device = lambda y, x, z, core: (y * 4 + x, z * 2 + core)
    sibling = device(y, x, z, 1 - core)
    turn = lambda value, step: lax.rem(value + step, 4)
    along_first = lambda j: device(turn(y, j * (1 - core)), x, turn(z, j * core), core)
    along_second = lambda j: device(turn(y, j * core), x, turn(z, j * (1 - core)), core)
    along_x = lambda j: device(y, turn(x, j), z, core)
    up = (lax.rem(row + mesh_rows - 1, mesh_rows), col)
    down = (lax.rem(row + 1, mesh_rows), col)
    before_me = (row, lax.rem(col + mesh_cols - 1, mesh_cols))
    after_me = (row, lax.rem(col + 1, mesh_cols))
    down_right = (down[0], after_me[1])
    up_left = (up[0], before_me[1])
    links = Links(send, recv)

    loads = [
        pltpu.make_async_copy(tile.at[:, :, pl.ds(j * SIDE, SIDE)], ext.at[j], local.at[j])
        for j in range(chunks)
    ]
    kept = slots - 1
    for b in range(batches):
        mine = pl.ds(b * slots, kept)
        loads.append(pltpu.make_async_copy(pats_in.at[mine], raw.at[mine], local.at[chunks + 2 + b]))
    loads.append(pltpu.make_async_copy(probe_in, probe.at[0], local.at[chunks + 1]))
    for load in loads:
        load.start()
    barrier = pltpu.get_barrier_semaphore()
    peers = [sibling, up, down, before_me, after_me, down_right, up_left]
    peers += [f(j) for f in (along_first, along_second, along_x) for j in (1, 2, 3)]
    for peer in peers:
        pl.semaphore_signal(barrier, inc=1, device_id=peer, device_id_type=MESH)
    pl.semaphore_wait(barrier, len(peers))

    rows, cols = iotas()
    infos = [
        links.copy(spots, theirs_info.at[i], peer) for i, peer in enumerate((down, after_me, down_right))
    ]
    parts = [pl.ds(0, HALF), pl.ds(HALF, HALF)]
    rims = [links.copy(tile.at[:, p, pl.ds(0, SIDE)], rim_in.at[:, p, :], before_me) for p in parts]

    def hand(b):
        return links.copy(pats_in.at[b * slots + kept], raw.at[b * slots + kept], down)

    handed = [hand(0)]
    sent = infos + rims

    def spot(b, who, s):
        read = (lambda i: spots[i]) if who == 0 else (lambda i: theirs_info[who - 1, i])
        r = lax.rem(read(2 * (b * slots + s)), SIDE)
        c = lax.rem(read(2 * (b * slots + s) + 1), SIDE * chunks)
        live = (s < read(2 * batches * slots + b)) * 1
        return lax.div(c, SIDE), r, lax.rem(c, SIDE), live

    def where_to(b, who, s, rows_below):
        k, r, cm, live = spot(b, who, s)
        inside = (rows < r) if rows_below else (rows >= r)
        return jnp.where(inside & (live == 1), k + (cols < cm).astype(jnp.int32), -1)

    def start_halos(b):
        return [
            links.copy(ext.at[pl.ds(0, chunks), :, pl.ds(SIDE - 8, 8), :], above.at[b], down),
            links.copy(ext.at[pl.ds(0, chunks), :, pl.ds(0, 8), :], below.at[b], up),
            links.copy(ext.at[chunks - 1, :, :, pl.ds(HALF, HALF)], before.at[b], after_me),
        ]

    def slot_copy(b, s, kind, away, there=None):
        src, dst = (rolled, arrived) if kind == 0 else (grads, gained)
        step = (1 - away) * (mesh_rows - 2) if kind == 0 else away * (mesh_rows - 2)
        i = (2 * b + kind) * slots + s
        return pltpu.make_async_remote_copy(
            src_ref=src.at[s] if there is None else src.at[s, :, there, :],
            dst_ref=dst.at[b, s] if there is None else dst.at[b, s, :, there, :],
            send_sem=slot_send.at[i],
            recv_sem=slot_recv.at[i],
            device_id=(lax.rem(row + 1 + step, mesh_rows), col),
            device_id_type=MESH,
        )

    def start_rim(b, s, part=None):
        away = int(s == kept)
        k, r, cm, live = spot(b, 1 - away, s)
        there = pl.ds(0, SIDE) if part is None else parts[part]
        right_of = (cols if part is None else cols[:HALF]) >= cm
        for plane in range(2):
            if part is None:
                after = ext[k + 1, plane, there]
            else:
                inside = ext[jnp.minimum(k + 1, chunks - 1), plane, there]
                after = jnp.where(k == chunks - 1, rim_in[plane, there], inside)
            rolled[s, plane, there] = jnp.where(right_of, ext[k, plane, there], after)
        slot_copy(b, s, 0, away, there).start()

    def order_patterns(b):
        def one(i, carry):
            high, low = split(raw[i])
            value = dot(perm[0], high) + dot(perm[0], low)
            high, low = split(value)
            pats[i] = dot(high, perm[1]) + dot(low, perm[1])
            return carry

        lax.fori_loop(b * slots, (b + 1) * slots, one, 0)

    def weigh(b):
        power = probe[b, 0] * probe[b, 0]
        for plane in range(1, 2 * MODES):
            power = power + probe[b, plane] * probe[b, plane]
        window[0] = power
        weight[...] = jnp.zeros_like(weight)

        def one(s, carry):
            for who in range(4):
                value = roll2(window[0], *spot(b, who, s)[1:3])
                chunk = where_to(b, who, s, who % 2 == 1)
                if who < 2:
                    for j in range(chunks):
                        weight[j] += jnp.where(chunk == j, value, 0.0)
                else:
                    weight[0] += jnp.where(chunk == chunks, value, 0.0)
            return carry

        lax.fori_loop(0, slots, one, 0)

    def smooth(b, halos):
        for copy in halos:
            copy.wait_recv()
        for part in range(2):
            for j in range(chunks):
                here = ext[j, part]
                top = jnp.where(row > 0, above[b, j, part, 7:8, :], 0.0)
                bottom = jnp.where(row < mesh_rows - 1, below[b, j, part, 0:1, :], 0.0)
                if j > 0:
                    lhs = ext[j - 1, part, :, HALF:][:, HALF - 1 : HALF]
                else:
                    lhs = jnp.where(col > 0, before[b, part, :, HALF - 1 : HALF], 0.0)
                rhs = ext[j + 1, part, :, :HALF][:, 0:1]
                if j == chunks - 1:
                    rhs = jnp.where(col < mesh_cols - 1, rhs, 0.0)
                neighbours = jnp.where(rows == 0, top, pltpu.roll(here, 1, 0))
                neighbours += jnp.where(rows == SIDE - 1, bottom, pltpu.roll(here, SIDE - 1, 0))
                neighbours += jnp.where(cols == 0, lhs, pltpu.roll(here, 1, 1))
                neighbours += jnp.where(cols == SIDE - 1, rhs, pltpu.roll(here, SIDE - 1, 1))
                base[j, part] = here + (step_object * smoothing) * (neighbours - 4.0 * here)

    def run_slots(b):
        pg[...] = jnp.zeros_like(pg)

        def one(i, carry):
            s = lax.rem(2 * i, slots)
            away = lax.rem(i, 2)
            slot_copy(b, s, 0, away).wait_recv()
            k, r, cm, live = [jnp.where(away == 1, t, o) for o, t in zip(spot(b, 0, s), spot(b, 1, s))]
            alive = live.astype(f32)
            here = (rows - r) * (1 - 2 * away) - away >= 0
            for part in range(2):
                own = jnp.where(cols >= cm, ext[k, part], ext[k + 1, part])
                value = jnp.where(here, own, arrived[b, s, part])
                window[part] = roll2(value, lax.rem(SIDE - r, SIDE), lax.rem(SIDE - cm, SIDE))

            def rows_in(m):
                pr, pi, xr, xi = probe[b, 2 * m], probe[b, 2 * m + 1], window[0], window[1]
                wr, wi = pr * xr - pi * xi, pr * xi + pi * xr
                middle[m, 0] = left(mats, 0, cat(0, wr[:HALF] + wr[HALF:], wi[:HALF] + wi[HALF:]))
                middle[m, 1] = left(mats, 4, cat(0, wr[:HALF] - wr[HALF:], wi[:HALF] - wi[HALF:]))

            def cols_in(pair):
                sums, diffs = [], []
                for m in pair:
                    for q in range(2):
                        value = middle[m, q]
                        tr, ti = value[:HALF], value[HALF:]
                        sums.append(cat(1, tr[:, :HALF] + tr[:, HALF:], ti[:, :HALF] + ti[:, HALF:]))
                        diffs.append(cat(1, tr[:, :HALF] - tr[:, HALF:], ti[:, :HALF] - ti[:, HALF:]))
                for q, (values, index) in enumerate(((sums, 2), (diffs, 6))):
                    far = right(cat(0, *values), mats, index)
                    for j, m in enumerate(pair):
                        value = far[j * SIDE : (j + 1) * SIDE]
                        psi[m, q] = value
                        total[q] = value * value if m == 0 else total[q] + value * value

            def cols_out(pair):
                ue = right(cat(0, *[psi[m, 0] * total[0] for m in pair]), mats, 0)
                uo = right(cat(0, *[psi[m, 1] * total[1] for m in pair]), mats, 4)
                for j, m in enumerate(pair):
                    e, o = ue[j * SIDE : (j + 1) * SIDE], uo[j * SIDE : (j + 1) * SIDE]
                    plus, minus = e + o, e - o
                    tr, ti = cat(1, plus[:, :HALF], minus[:, :HALF]), cat(1, plus[:, HALF:], minus[:, HALF:])
                    middle[m, 0], middle[m, 1] = cat(0, tr[:HALF], ti[:HALF]), cat(0, tr[HALF:], ti[HALF:])

            def rows_out(m):
                ze, zo = left(mats, 2, middle[m, 0]), left(mats, 6, middle[m, 1])
                plus, minus = ze + zo, ze - zo
                br, bi = cat(0, plus[:HALF], minus[:HALF]), cat(0, plus[HALF:], minus[HALF:])
                pr, pi, xr, xi = probe[b, 2 * m], probe[b, 2 * m + 1], window[0], window[1]
                gr, gi = pr * br + pi * bi, pr * bi - pi * br
                grads[s, 0] = gr if m == 0 else grads[s, 0] + gr
                grads[s, 1] = gi if m == 0 else grads[s, 1] + gi
                pg[1 + 2 * m] += xr * br + xi * bi
                pg[2 + 2 * m] += xr * bi - xi * br

            pairs = [tuple(range(m, m + 2)) for m in range(0, MODES, 2)]
            for m in pairs[0]:
                rows_in(m)
            for p, pair in enumerate(pairs):
                for m in pairs[p + 1] if p + 1 < len(pairs) else ():
                    rows_in(m)
                cols_in(pair)
            for q in range(2):
                value = total[q]
                value = value[:, :HALF] + value[:, HALF:] - pats[b * slots + s, :, pl.ds(q * HALF, HALF)]
                total[q] = cat(1, value, value) * alive
            cols_out(pairs[0])
            for p, pair in enumerate(pairs):
                if p + 1 < len(pairs):
                    cols_out(pairs[p + 1])
                for m in pair:
                    rows_out(m)
            pg[0] += (window[0] * window[0] + window[1] * window[1]) * alive
            for part in range(2):
                grads[s, part] = roll2(grads[s, part], r, cm)
            slot_copy(b, s, 1, away).start()
            return carry

        lax.fori_loop(0, slots, one, 0)

    def gather(b, s):
        away = int(s == kept)
        slot_copy(b, s, 1, away).wait_recv()
        own, theirs = where_to(b, 0, s, False), where_to(b, 1, s, True)
        mine, others = (gained.at[b, s], grads.at[s]) if away else (grads.at[s], gained.at[b, s])
        for part in range(2):
            for j in range(chunks + 1):
                value = jnp.where(own == j, mine[part], 0.0) + jnp.where(theirs == j, others[part], 0.0)
                if s == 0:
                    acc[j, part] = value
                else:
                    acc[j, part] += value

    groups = [pl.ds(0, 1 + MODES), pl.ds(1 + MODES, MODES)]

    def reduce_cores(g):
        theirs = at((1 - core) * HALF, 0, HALF)
        one = links.copy(pg.at[groups[g], theirs, :], got1.at[groups[g]], sibling)
        sent.append(one)
        return [one]

    def reduce_first(g, ones):
        twos = []
        for copy in ones:
            copy.wait_recv()
        for step in (2, 1, 3, 0):
            piece = turn(first, step)
            mine, there = at(core * HALF, piece, 32), at(0, piece, 32)
            half[groups[g], there, :] = pg[groups[g], mine, :] + got1[groups[g], there, :]
            if step:
                src, dst = half.at[groups[g], there, :], got2.at[step - 1, groups[g]]
                twos.append(links.copy(src, dst, along_first(step)))
        sent.extend(twos)
        return twos

    def reduce_second(g, twos):
        threes, planes = [], groups[g]
        for copy in twos:
            copy.wait_recv()
        for step in (2, 1, 3, 0):
            piece = turn(second, step)
            there, within = at(first * 32, piece, 8), at(0, piece, 8)
            value = half[planes, there, :] + got2[0, planes, within, :]
            half[planes, there, :] = value + got2[1, planes, within, :] + got2[2, planes, within, :]
            if step:
                src, dst = half.at[planes, there, :], got3.at[step - 1, planes]
                threes.append(links.copy(src, dst, along_second(step)))
        sent.extend(threes)
        return threes

    def reduce_x(g, threes):
        fours, planes = [], groups[g]
        for copy in threes:
            copy.wait_recv()
        there = at(first * 32, second, 8)
        got4[x, planes] = half[planes, there, :] + got3[0, planes] + got3[1, planes] + got3[2, planes]
        for step in (2, 1, 3):
            fours.append(links.copy(got4.at[x, planes], got4.at[x, planes], along_x(step)))
        sent.extend(fours)
        return fours

    def spread(b, g, block, peers):
        planes = probe.at[b + 1, pl.ds(g * MODES, MODES)]
        copies = [links.copy(planes.at[:, block, :], planes.at[:, block, :], peer) for peer in peers]
        sent.extend(copies)
        return copies

    def spread_second(b, g, fours):
        for copy in fours:
            copy.wait_recv()
        mine = at(core * HALF + first * 32, second, 8)
        scale = step_probe / (got4[0, 0] + got4[1, 0] + got4[2, 0] + got4[3, 0] + probe_floor)
        for plane in range(g * MODES, (g + 1) * MODES):
            grad = got4[0, plane + 1] + got4[1, plane + 1] + got4[2, plane + 1] + got4[3, plane + 1]
            probe[b + 1, plane, mine, :] = probe[b, plane, mine, :] - scale * grad
        return spread(b, g, mine, [along_second(step) for step in (2, 1, 3)])

    def spread_first(b, g, copies):
        for copy in copies:
            copy.wait_recv()
        return spread(b, g, at(core * HALF, first, 32), [along_first(step) for step in (2, 1, 3)])

    def spread_cores(b, g, copies):
        for copy in copies:
            copy.wait_recv()
        return spread(b, g, at(core * HALF, 0, HALF), [sibling])

    for load in loads[:chunks]:
        load.wait()
    halos = start_halos(0)
    for load in loads[chunks:]:
        load.wait()
    for copy in infos:
        copy.wait_recv()
    for part in range(2):
        rims[part].wait_recv()
        start_rim(0, 0, part)
    ext[chunks] = rim_in[...]
    start_rim(0, kept)
    handed += [hand(b) for b in range(1, batches)]
    sent += handed
    both = range(2)
    got1s, got2s, got3s, got4s = got1, got2, got3, got4
    stores = []
    for b in range(batches):
        more = b + 1 < batches
        got1, got2, got3, got4 = got1s.at[b], got2s.at[b], got3s.at[b], got4s.at[b]
        if b == 0:
            handed[0].wait_recv()
            order_patterns(0)
            smooth(0, halos)
        if more:
            weigh(b)
            sides = [
                links.copy(base.at[0], side.at[pl.ds(0, 2)], before_me),
                links.copy(weight.at[0], side.at[2], before_me),
            ]
        if b == 0:
            slot_copy(b, 0, 0, 0).wait_send()
            for s in range(1, kept):
                start_rim(b, s)
        run_slots(b)
        ones = [reduce_cores(g) for g in both]
        twos = [reduce_first(g, ones[g]) for g in both]
        gather(b, 0)
        if not more:
            weigh(b)
        gather(b, kept)
        threes = [reduce_second(g, twos[g]) for g in both]
        for s in range(1, kept):
            gather(b, s)
        to_right = links.copy(acc.at[chunks], from_left.at[b], after_me)
        sent.append(to_right)
        if more:
            to_left = links.copy(acc.at[0], from_right, before_me)
            sent.append(to_left)
        fours = [reduce_x(g, threes[g]) for g in both]
        for copy in halos:
            copy.wait_send()
        for j in list(range(1, chunks)) + [0]:
            if j == 0:
                fives = [spread_second(b, g, fours[g]) for g in both]
                to_right.wait_recv()
            scale = step_object / (weight[j] + object_floor)
            for part in range(2):
                value = acc[j, part] + from_left[b, part] if j == 0 else acc[j, part]
                ext[j, part] = base[j, part] - scale * value
            if not more:
                store = pltpu.make_async_copy(ext.at[j], out_tile.at[:, :, pl.ds(j * SIDE, SIDE)], local.at[j])
                store.start()
                stores.append(store)
        for s in range(slots):
            away = int(s == kept)
            if s:
                slot_copy(b, s, 0, away).wait_send()
            slot_copy(b, s, 1, away).wait_send()
        if more:
            to_left.wait_recv()
            for copy in sides:
                copy.wait_recv()
            scale = step_object / (side[2] + object_floor)
            for part in range(2):
                ext[chunks, part] = side[part] - scale * (acc[chunks, part] + from_right[part])
            start_rim(b + 1, 0)
            start_rim(b + 1, kept)
            halos = start_halos(b + 1)
        sixes = [spread_first(b, g, fives[g]) for g in both]
        if more:
            for copy in sides:
                copy.wait_send()
            handed[b + 1].wait_recv()
            order_patterns(b + 1)
            smooth(b + 1, halos)
        sevens = [spread_cores(b, g, sixes[g]) for g in both]
        if more:
            slot_copy(b + 1, 0, 0, 0).wait_send()
            for s in range(1, kept):
                start_rim(b + 1, s)
        for copies in sevens:
            for copy in copies:
                copy.wait_recv()
        if more:
            for copy in sent:
                copy.wait_send()
            sent.clear()
    last = pltpu.make_async_copy(probe.at[batches], out_probe, local.at[chunks + 1])
    last.start()
    for copy in sent:
        copy.wait_send()
    for store in stores + [last]:
        store.wait()


def shards(object_field, probe_modes, offsets, live_counts, patterns):
    tile_rows, tile_cols = object_field.shape[1:]
    chunks = tile_cols // SIDE
    batches, slots = offsets.shape[:2]
    mesh_rows, mesh_cols = lax.axis_size("row"), lax.axis_size("col")
    spots = jnp.concatenate([offsets.reshape(-1), live_counts.reshape(-1)])
    spots = jnp.pad(spots, (0, 128 - spots.shape[0]))
    perm = np.zeros((SIDE, SIDE), np.float32)
    j = np.arange(SIDE)
    perm[j, (j % 2) * HALF + j // 2] = 1.0
    perm = jnp.asarray(np.stack([perm.T, perm]), jnp.bfloat16)

    vmem, hbm = pl.BlockSpec(memory_space=VMEM), pl.BlockSpec(memory_space=pl.ANY)
    block = (2, SIDE, SIDE)
    buf = lambda *shape: pltpu.VMEM(shape, f32)
    dma = pltpu.SemaphoreType.DMA
    tile, probe = pl.pallas_call(
        functools.partial(whole_kernel, batches, slots, chunks, mesh_rows, mesh_cols),
        in_specs=[pl.BlockSpec(memory_space=pltpu.SMEM), hbm, hbm, hbm, vmem, vmem],
        out_specs=[hbm, hbm],
        out_shape=[
            jax.ShapeDtypeStruct(object_field.shape, f32),
            jax.ShapeDtypeStruct((2 * MODES, SIDE, SIDE), f32),
        ],
        scratch_shapes=[
            pltpu.SMEM((3, 128), jnp.int32),
            buf(chunks + 1, *block),
            buf(*block),
            buf(batches + 1, 2 * MODES, SIDE, SIDE),
            buf(batches * slots, SIDE, SIDE),
            buf(batches * slots, SIDE, SIDE),
            buf(slots, *block),
            buf(batches, slots, *block),
            buf(slots, *block),
            buf(batches, slots, *block),
            buf(chunks + 1, *block),
            buf(chunks, *block),
            buf(chunks, SIDE, SIDE),
            buf(3, SIDE, SIDE),
            buf(batches, *block),
            buf(*block),
            buf(batches, chunks, 2, 8, SIDE),
            buf(batches, chunks, 2, 8, SIDE),
            buf(batches, 2, SIDE, HALF),
            buf(MODES, *block),
            buf(MODES, *block),
            buf(*block),
            buf(*block),
            buf(PLANES, SIDE, SIDE),
            buf(batches, PLANES, HALF, SIDE),
            buf(PLANES, HALF, SIDE),
            buf(batches, 3, PLANES, 32, SIDE),
            buf(batches, 3, PLANES, 8, SIDE),
            buf(batches, 4, PLANES, 8, SIDE),
            dma((110,)),
            dma((110,)),
            dma((2 * batches * slots,)),
            dma((2 * batches * slots,)),
            dma((chunks + 2 + batches,)),
        ],
        compiler_params=pltpu.CompilerParams(
            collective_id=0, has_side_effects=True, vmem_limit_bytes=60 * 2**20
        ),
        name="reconstruct",
    )(
        spots,
        object_field,
        probe_modes.reshape(2 * MODES, SIDE, SIDE),
        patterns.reshape(batches * slots, SIDE, SIDE),
        jnp.asarray(matrices()),
        perm,
    )
    return (tile, probe.reshape(probe_modes.shape))


def solution(mesh):
    placed = (
        P(None, "row", "col"),
        P(),
        P(None, ("row", "col"), None),
        P(None, ("row", "col")),
        P(None, ("row", "col"), None, None),
    )
    return jax.shard_map(
        shards, mesh=mesh, in_specs=placed, out_specs=(P(None, "row", "col"), P()), check_vma=False
    )
```
